128 devices in a mesh: stack: 8 (over y, core), cls: 16 (over z, x).
Axes of the slice: x: 4, y: 4, z: 4, core: 2. Of those that a mesh axis runs over, the one named last changes fastest.
Arguments:
- particles: bfloat16 [8192, 256, 256], P(('stack', 'cls')), may hold values from -64 to 64
- classes: int32 [8192], P(('stack', 'cls')), may hold values from 0 to 511, as said below
- angles: int32 [8192], P(('stack', 'cls')), may hold values from 0 to 15
- groups: int32 [8192], P(('stack', 'cls')), may hold values from 0 to 15
- posterior: bfloat16 [8192, 2], P(('stack', 'cls')), may hold values from 0.099609375 to 1
- left_maps: bfloat16 [16, 256, 256], replicated, may hold values from -0.375 to 0.375
- right_maps: bfloat16 [16, 256, 256], replicated, may hold values from -0.375 to 0.375
- ctf_table: float32 [16, 256, 256], replicated, may hold values from -1 to 1
Outputs:
- class_sums: float32 [512, 256, 256], P('cls', 'stack')
- class_weights: float32 [512, 256, 256], P('cls', 'stack')
- class_norms: float32 [512], P('cls')
The draws below stay inside these ranges and needn't reach their ends.
Inputs may be any that keep to these rules, and one draw needn't show every extreme that they name: Owner k holds classes k * 32 to (k + 1) * 32 - 1. Among the particles of one device at most 8 belong to one owner's classes; some owner gets exactly 8 from every device.
All inputs are finite; a program needn't handle non-finite values.
Results may differ from the reference program's by a relative error of at most 0.0029.
Values may be sent and summed in bfloat16 or wider, within the bound.
A program may use at most 192 MiB of HBM per device.

```python
import math
import jax
import jax.numpy as jnp
from jax import lax

L = 256
CLS_LOC = 32
GROUPS = 16
ANGLES = 16
NEAR = 2
P_DEV = 64
CAP = 8
NPART = 8192
CLASSES = 512
N_STACK = 8
N_CLS = 16


def draw_particles(key, part):
    key = jax.random.fold_in(key, 11)
    noise_key, scale_key = jax.random.split(key, 2)
    position = jnp.arange(NPART, dtype=jnp.float32)
    scales = jnp.sqrt(1.0 + 2.0 * position / NPART) * 10.0 ** jax.random.uniform(scale_key, (NPART,), jnp.float32, -1.0, 0.0)
    noise = jax.random.normal(noise_key, (NPART, L, L), jnp.float32)
    return (noise * scales[:, None, None]).astype(jnp.bfloat16)


def draw_classes(key, part):
    key = jax.random.fold_in(key, 23)
    hot_key, offset_key, perm_key, member_key = jax.random.split(key, 4)
    blocks_count = N_STACK * N_CLS
    hot_owner = jax.random.randint(hot_key, (), 0, N_CLS)
    offsets = jax.random.randint(offset_key, (blocks_count, 1), 0, max(N_CLS - 1, 1))
    within = jnp.arange(P_DEV, dtype=jnp.int32)[None, :]
    others = (hot_owner + 1 + (within - CAP + offsets) % max(N_CLS - 1, 1)) % N_CLS
    owners = jnp.where(within < CAP, hot_owner, others)
    perm_keys = jax.random.split(perm_key, blocks_count)
    shuffles = jax.vmap(lambda single: jax.random.permutation(single, P_DEV))(perm_keys)
    owners = jnp.take_along_axis(owners, shuffles, 1)
    members = jax.random.randint(member_key, (blocks_count, P_DEV), 0, CLS_LOC)
    return (owners * CLS_LOC + members).reshape(-1).astype(jnp.int32)


def place_ends(values, rng, smallest, high):
    place = [jax.random.randint(jax.random.fold_in(rng, axis), (), 0, length) for axis, length in enumerate(values.shape)]
    widest = values.shape.index(max(values.shape))
    beside = place[:widest] + [(place[widest] + 1) % values.shape[widest]] + place[widest + 1:]
    return values.at[tuple(place)].set(smallest).at[tuple(beside)].set(high)


def level_of(key, extent, shards, smallest, largest):
    def one(dim, blocks):
        draws = jax.random.uniform(jax.random.fold_in(jax.random.fold_in(key, 6), dim), (blocks,), jnp.float32, smallest / len(shards), largest / len(shards))
        return jnp.repeat(jnp.exp(draws), extent[dim] // blocks).reshape((-1,) + (1,) * (len(extent) - dim - 1))

    loudness = one(*shards[0])
    for cut in shards[1:]:
        loudness = loudness * one(*cut)
    return loudness


def gaussian(own_key, extent, spread, most, held_as=jnp.bfloat16):
    entries = spread * jax.random.normal(own_key, extent, jnp.float32)
    return jnp.clip(entries, min=-most, max=most).astype(held_as)


def setup_inputs(seed: int = 0) -> dict:
    key_of = jax.random.split(jax.random.key(seed), 9)
    particles = draw_particles(jax.random.fold_in(key_of[8], 71), 0)
    classes = draw_classes(jax.random.fold_in(key_of[8], 71), 0)
    angles = place_ends(jax.random.randint(key_of[2], (NPART,), 0, ANGLES), jax.random.fold_in(key_of[2], 1), 0, ANGLES - 1).astype(jnp.int32)
    groups = place_ends(jax.random.randint(key_of[3], (NPART,), 0, GROUPS), jax.random.fold_in(key_of[3], 1), 0, GROUPS - 1).astype(jnp.int32)
    posterior = jnp.clip(jnp.exp(math.log(1.0) - 2.306499 * jax.random.uniform(key_of[4], (NPART, NEAR), jnp.float32) ** level_of(key_of[4], (NPART, NEAR), ((0, 128),), -0.2, 0.2)), 0.099609375, 1.0).astype(jnp.bfloat16)
    left_maps = gaussian(key_of[5], (ANGLES, L, L), L ** -0.5, 0.375)
    right_maps = gaussian(key_of[6], (ANGLES, L, L), L ** -0.5, 0.375)
    ctf_table = jnp.clip(jax.random.uniform(key_of[7], (GROUPS, L, L), jnp.float32, -1.0, 1.0), -1.0, 1.0)
    return dict(particles=particles, classes=classes, angles=angles, groups=groups, posterior=posterior, left_maps=left_maps, right_maps=right_maps, ctf_table=ctf_table)


def reference(particles, classes, angles, groups, posterior, left_maps, right_maps, ctf_table):
    block_size = min(64, NPART)
    blocks_count = NPART // block_size
    zero_images = jnp.zeros((CLASSES, L, L), jnp.float32)
    zero_norms = jnp.zeros((CLASSES,), jnp.float32)

    def accumulate(totals, block_index):
        class_total, weight_total, power_total = totals
        begin = (block_index * block_size).astype(jnp.int32)

        def cut(array):
            return lax.dynamic_slice_in_dim(array, begin, block_size, 0)

        block_images = cut(particles).astype(jnp.float32)
        labels = cut(classes)
        turns = cut(angles)
        defocus = cut(groups)
        weights_in = cut(posterior).astype(jnp.float32)
        combined = jnp.zeros((block_size, L, L), jnp.float32)
        for nearby in range(NEAR):
            turn_now = (turns + nearby) % ANGLES
            right_now = right_maps[turn_now].astype(jnp.float32)
            left_now = left_maps[turn_now].astype(jnp.float32)
            sheared = jnp.einsum("bij,bkj->bik", block_images, right_now).astype(jnp.bfloat16)
            sheared = lax.optimization_barrier(sheared).astype(jnp.float32)
            rotated = jnp.einsum("bij,bjk->bik", left_now, sheared)
            combined = combined + weights_in[:, nearby][:, None, None] * rotated
        contrast = ctf_table[defocus]
        weighted = contrast * combined
        class_total = class_total.at[labels].add(weighted)
        weight_total = weight_total.at[labels].add(jnp.sum(weights_in, 1)[:, None, None] * contrast * contrast)
        power_total = power_total.at[labels].add(jnp.mean(weighted * weighted, axis=(1, 2)))
        return (class_total, weight_total, power_total), None

    totals, unused = lax.scan(accumulate, (zero_images, zero_images, zero_norms), jnp.arange(blocks_count, dtype=jnp.int32))
    return totals[0], totals[1], totals[2]
```

```python
import jax
import jax.numpy as jnp
from jax import lax
from jax.experimental import pallas as pl
from jax.experimental.pallas import tpu as pltpu
from jax.sharding import PartitionSpec as P

MESH = pl.DeviceIdType.MESH
F32 = jnp.float32
BF16 = jnp.bfloat16
SIDE = 256
ANGLES = 16
GROUPS = 16
LOCAL = 64
BATCH = 16
BATCHES = LOCAL // BATCH
STACK = 8
OWNERS = 16
CLS_LOC = 32
CLASSES = OWNERS * CLS_LOC
ROWS = SIDE // STACK
PEOPLE = STACK * LOCAL
PITCH = SIDE + 8
LANES = 128
CHUNKS = (8, 8, 4, 4, 4, 2, 2)
STARTS = tuple(sum(CHUNKS[:n]) for n in range(len(CHUNKS)))
NCHUNK = len(CHUNKS)
STACK_STEPS = tuple((dy, dc) for dy in (2, 1, 3, 0) for dc in (0, 1) if (dy, dc) != (0, 0))
NT = (((1,), (1,)), ((), ()))


def body(
    angles, groups, posterior, tile, particles, left_hbm, right_hbm, ctf_hbm,
    sums_out, weights_out, norms_out,
    left, right, ctf, images, weighted, power, outgoing, gathered,
    hot_a, hot_b, mixed, tiles, norm_tile, norm_tiles,
    partial, first_in, second, second_in,
    small, small_first, small_mid, small_second,
    load_sem, image_sem, own_sem,
    tile_send, tile_recv, norm_send, norm_recv,
    early_send, early_recv, y_send, y_recv,
    first_send, first_recv, second_send, second_recv,
    small_send, small_recv,
):
    s = lax.axis_index("stack")
    k = lax.axis_index("cls")
    y, core = s // 2, s % 2
    z, x = k // 4, k % 4

    def along_stack(step):
        return (((y + step[0]) % 4) * 2 + (core + step[1]) % 2, k)

    def along_x(d):
        return (s, z * 4 + (x + d) % 4)

    def along_z(d):
        return (s, ((z + d) % 4) * 4 + x)

    loads = [
        pltpu.make_async_copy(left_hbm, left, load_sem.at[0]),
        pltpu.make_async_copy(right_hbm, right, load_sem.at[1]),
        pltpu.make_async_copy(ctf_hbm, ctf, load_sem.at[2]),
    ]

    def image_load(b):
        return pltpu.make_async_copy(
            particles.at[pl.ds(b * BATCH, BATCH)], images.at[b % 2], image_sem.at[b % 2]
        )

    loads[1].start()
    image_load(0).start()
    loads[0].start()
    loads[2].start()
    image_load(1).start()

    barrier = pltpu.get_barrier_semaphore()
    peers = [along_stack(step) for step in STACK_STEPS]
    peers += [along_x(d) for d in (1, 2, 3)] + [along_z(d) for d in (1, 2, 3)]
    for peer in peers:
        pl.semaphore_signal(barrier, inc=1, device_id=peer, device_id_type=MESH)

    def remote(src, dst, send, recv, peer):
        return pltpu.make_async_remote_copy(
            src_ref=src, dst_ref=dst, send_sem=send, recv_sem=recv, device_id=peer, device_id_type=MESH
        )

    def tile_copies():
        return [
            remote(tile, tiles.at[s], tile_send.at[n], tile_recv.at[n], along_stack(step))
            for n, step in enumerate(STACK_STEPS)
        ]

    def norm_copies():
        return [
            remote(norm_tile, norm_tiles.at[s], norm_send.at[n], norm_recv.at[n], along_stack(step))
            for n, step in enumerate(STACK_STEPS)
        ]

    def early_copies(b):
        rows = CHUNKS[0]
        out = []
        for n, step in enumerate(STACK_STEPS):
            peer = along_stack(step)
            out.append(
                remote(
                    outgoing.at[pl.ds(peer[0] * ROWS, rows), pl.ds(b * BATCH, BATCH)],
                    gathered.at[pl.ds(0, rows), pl.ds(s * LOCAL + b * BATCH, BATCH)],
                    early_send.at[b, n], early_recv.at[b, n], peer,
                )
            )
        return out

    def y_copies(c):
        start, rows = STARTS[c], CHUNKS[c]
        out = []
        for n, step in enumerate(STACK_STEPS):
            peer = along_stack(step)
            out.append(
                remote(
                    outgoing.at[pl.ds(peer[0] * ROWS + start, rows)],
                    gathered.at[pl.ds(start, rows), pl.ds(s * LOCAL, LOCAL)],
                    y_send.at[c, n], y_recv.at[c, n], peer,
                )
            )
        return out

    def own_copy(c):
        start, rows = STARTS[c], CHUNKS[c]
        return pltpu.make_async_copy(
            outgoing.at[pl.ds(s * ROWS + start, rows)],
            gathered.at[pl.ds(start, rows), pl.ds(s * LOCAL, LOCAL)],
            own_sem.at[c],
        )

    def first_copies(c):
        half = CHUNKS[c] // 2
        out = []
        for d in (1, 2, 3):
            for part, (hop, spot) in enumerate(((along_x, (x + d) % 4), (along_z, (z + d) % 4))):
                rows = pl.ds(STARTS[c] + part * half, half)
                out.append(
                    remote(
                        partial.at[rows, pl.ds(spot * 128, 128)], first_in.at[d - 1, rows],
                        first_send.at[c, part, d - 1], first_recv.at[c, part, d - 1], hop(d),
                    )
                )
        return out

    def second_copies(c):
        half = CHUNKS[c] // 2
        out = []
        for d in (1, 2, 3):
            for part, (hop, spot) in enumerate(((along_z, (z + d) % 4), (along_x, (x + d) % 4))):
                rows = pl.ds(STARTS[c] + part * half, half)
                out.append(
                    remote(
                        second.at[rows, pl.ds(spot * CLS_LOC, CLS_LOC)], second_in.at[d - 1, rows],
                        second_send.at[c, part, d - 1], second_recv.at[c, part, d - 1], hop(d),
                    )
                )
        return out

    def small_first_copies():
        return [
            remote(
                small.at[pl.ds(((x + d) % 4) * 128, 128)], small_first.at[d - 1],
                small_send.at[0, d - 1], small_recv.at[0, d - 1], along_x(d),
            )
            for d in (1, 2, 3)
        ]

    def small_second_copies():
        return [
            remote(
                small_mid.at[pl.ds(((z + d) % 4) * CLS_LOC, CLS_LOC)], small_second.at[d - 1],
                small_send.at[1, d - 1], small_recv.at[1, d - 1], along_z(d),
            )
            for d in (1, 2, 3)
        ]

    def start(copies):
        for copy in copies:
            copy.start()

    def arrive(copies):
        for copy in copies:
            copy.wait_recv()

    def leave(copies):
        for copy in copies:
            copy.wait_send()

    for b in range(BATCHES):
        if b == 0:
            loads[1].wait()
        image_load(b).wait()
        if b == 0:
            loads[0].wait()
            loads[2].wait()

        def one(i, carry, b=b):
            p = b * BATCH + i
            turn = angles[p]
            after = (turn + 1) & (ANGLES - 1)
            image = images[b % 2, i]
            low = lax.dot_general(image, right[turn], NT, preferred_element_type=F32).astype(BF16)
            high = lax.dot_general(image, right[after], NT, preferred_element_type=F32).astype(BF16)
            spun = posterior[2 * p] * jnp.dot(left[turn], low, preferred_element_type=F32)
            spun += posterior[2 * p + 1] * jnp.dot(left[after], high, preferred_element_type=F32)
            spun = ctf[groups[p]] * spun
            weighted[0, pl.ds(i * PITCH, SIDE), :] = spun[:, :LANES]
            weighted[1, pl.ds(i * PITCH, SIDE), :] = spun[:, LANES:]
            squares = jnp.sum(spun * spun, axis=0, keepdims=True)
            power[pl.ds(p, 1), :] = squares[:, :LANES] + squares[:, LANES:]
            return carry

        lax.fori_loop(0, BATCH, one, 0)
        if b + 2 < BATCHES:
            image_load(b + 2).start()

        def turn_over(r, carry, b=b):
            for h in range(2):
                lines = weighted[h, pl.ds(r, BATCH, stride=PITCH), :]
                outgoing[r, b * BATCH:(b + 1) * BATCH, h * LANES:(h + 1) * LANES] = lines.astype(BF16)
            return carry

        lax.fori_loop(0, SIDE, turn_over, 0, unroll=8)
        if b == 0:
            pl.semaphore_wait(barrier, len(peers))
            start(tile_copies())
        start(early_copies(b))

    start(y_copies(1))
    for c in range(NCHUNK):
        own_copy(c).start()

    tiles[s] = tile[...]
    lane = lax.broadcasted_iota(jnp.int32, (8, LANES), 1)
    own_power = jnp.sum(power[...], axis=1, keepdims=True) * (1.0 / (SIDE * SIDE))
    spot = lax.broadcasted_iota(jnp.int32, (LOCAL, LANES), 1) & (LOCAL - 1)
    line = lax.broadcasted_iota(jnp.int32, (LOCAL, LANES), 0)
    own_power = jnp.sum(jnp.where(spot == line, own_power, 0.0), axis=0, keepdims=True)
    norm_tile[...] = jnp.broadcast_to(own_power, (8, LANES))
    norm_tiles[s] = jnp.broadcast_to(own_power, (8, LANES))
    start(norm_copies())

    arrive(tile_copies())
    q = lax.broadcasted_iota(jnp.int32, (CLASSES, LANES), 0)
    swapped = (((q >> 5) & 3) * 4 + (q >> 7)) * CLS_LOC + (q & (CLS_LOC - 1))
    natural = q.astype(F32)
    swapped = swapped.astype(F32)
    which = lax.broadcasted_iota(jnp.int32, (LANES, LANES), 0)
    which_group = (which & (GROUPS - 1)).astype(F32)
    for j in range(STACK // 2):
        cols = slice(j * LANES, (j + 1) * LANES)
        both = jnp.where(lane < LOCAL, tiles[2 * j], tiles[2 * j + 1])
        hot_a[:, cols] = jnp.where(swapped == both[0:1], 1.0, 0.0).astype(BF16)
        hot_b[:, cols] = jnp.where(natural == both[0:1], 1.0, 0.0).astype(BF16)
        chance = jnp.where(which < GROUPS, both[2:3], both[3:4])
        keep = (which_group == both[1:2]) & (which < 2 * GROUPS)
        mixed[:, cols] = jnp.where(keep, chance, 0.0).astype(BF16)

    def small_start():
        arrive(norm_copies())
        total = jnp.zeros((CLASSES, LANES), F32)
        for j in range(STACK // 2):
            both = jnp.where(lane < LOCAL, tiles[2 * j], tiles[2 * j + 1])
            norm = jnp.where(lane < LOCAL, norm_tiles[2 * j], norm_tiles[2 * j + 1])
            total += jnp.where(swapped == both[0:1], norm[0:1], 0.0)
        small[:, 0:LANES] = total
        small[:, LANES:2 * LANES] = lax.dot_general(hot_a[...], mixed[...], NT, preferred_element_type=F32)
        start(small_first_copies())

    def small_middle():
        arrive(small_first_copies())
        small_mid[...] = (
            small[pl.ds(x * 128, 128), :] + small_first[0] + small_first[1] + small_first[2]
        )
        start(small_second_copies())

    def small_end():
        arrive(small_second_copies())
        total = small_mid[pl.ds(z * CLS_LOC, CLS_LOC), :] + small_second[0] + small_second[1] + small_second[2]
        norms = jnp.sum(total[:, :LANES], axis=1, keepdims=True)
        norms_out[...] = jnp.broadcast_to(norms, (CLS_LOC, LANES))
        coef = total[:, LANES:LANES + GROUPS] + total[:, LANES + GROUPS:LANES + 2 * GROUPS]

        def weigh(r, carry):
            lines = jnp.concatenate([ctf[g, pl.ds(s * ROWS + r, 1), :] for g in range(GROUPS)], axis=0)
            weights_out[r] = jnp.dot(
                coef, lines * lines, precision=lax.Precision.HIGHEST, preferred_element_type=F32
            )
            return carry

        lax.fori_loop(0, ROWS, weigh, 0)

    def by_class(c):
        half = CHUNKS[c] // 2
        for part, hot in enumerate((hot_a, hot_b)):

            def add(i, carry, part=part, hot=hot):
                r = STARTS[c] + part * half + i
                partial[r] = jnp.dot(hot[...], gathered[r], preferred_element_type=F32).astype(BF16)
                return carry

            lax.fori_loop(0, half, add, 0)

    def add_first(c):
        half = CHUNKS[c] // 2
        for part, mine in enumerate((x, z)):

            def add(i, carry, part=part, mine=mine):
                r = STARTS[c] + part * half + i
                total = partial[r, pl.ds(mine * 128, 128), :].astype(F32)
                for d in range(3):
                    total += first_in[d, r].astype(F32)
                second[r] = total
                return carry

            lax.fori_loop(0, half, add, 0)

    def add_second(c):
        half = CHUNKS[c] // 2
        for part, mine in enumerate((z, x)):

            def add(i, carry, part=part, mine=mine):
                r = STARTS[c] + part * half + i
                total = second[r, pl.ds(mine * CLS_LOC, CLS_LOC), :]
                for d in range(3):
                    total += second_in[d, r]
                sums_out[r] = total
                return carry

            lax.fori_loop(0, half, add, 0)

    for step in range(NCHUNK + 2):
        c = step
        if c + 2 < NCHUNK:
            start(y_copies(c + 2))
        if c < NCHUNK:
            if c == 0:
                for b in range(BATCHES):
                    arrive(early_copies(b))
            else:
                arrive(y_copies(c))
            own_copy(c).wait()
            by_class(c)
            start(first_copies(c))
        if c == 0:
            small_start()
        if c == 1:
            small_middle()
        if 0 <= c - 1 < NCHUNK:
            arrive(first_copies(c - 1))
            add_first(c - 1)
            start(second_copies(c - 1))
        if c == 2:
            small_end()
        if 0 <= c - 2 < NCHUNK:
            arrive(second_copies(c - 2))
            add_second(c - 2)

    leave(tile_copies())
    leave(norm_copies())
    for b in range(BATCHES):
        leave(early_copies(b))
    for c in range(NCHUNK):
        if c > 0:
            leave(y_copies(c))
        leave(first_copies(c))
        leave(second_copies(c))
    leave(small_first_copies())
    leave(small_second_copies())


def per_device(particles, classes, angles, groups, posterior, left_maps, right_maps, ctf_table):
    chances = posterior.astype(F32)
    tile = jnp.stack([classes.astype(F32), groups.astype(F32), chances[:, 0], chances[:, 1]], 0)
    tile = jnp.pad(jnp.concatenate([tile, tile], 1), ((0, 4), (0, 0)))
    smem = pl.BlockSpec(memory_space=pltpu.SMEM)
    vmem = pl.BlockSpec(memory_space=pltpu.VMEM)
    hbm = pl.BlockSpec(memory_space=pl.ANY)
    n = len(STACK_STEPS)
    dma = pltpu.SemaphoreType.DMA
    sums, weights, norms = pl.pallas_call(
        body,
        out_shape=(
            jax.ShapeDtypeStruct((ROWS, CLS_LOC, SIDE), F32),
            jax.ShapeDtypeStruct((ROWS, CLS_LOC, SIDE), F32),
            jax.ShapeDtypeStruct((CLS_LOC, LANES), F32),
        ),
        in_specs=[smem, smem, smem, vmem, hbm, hbm, hbm, hbm],
        out_specs=(vmem, vmem, vmem),
        scratch_shapes=[
            pltpu.VMEM((ANGLES, SIDE, SIDE), BF16),
            pltpu.VMEM((ANGLES, SIDE, SIDE), BF16),
            pltpu.VMEM((GROUPS, SIDE, SIDE), F32),
            pltpu.VMEM((2, BATCH, SIDE, SIDE), BF16),
            pltpu.VMEM((2, BATCH * PITCH, LANES), F32),
            pltpu.VMEM((LOCAL, LANES), F32),
            pltpu.VMEM((SIDE, LOCAL, SIDE), BF16),
            pltpu.VMEM((ROWS, PEOPLE, SIDE), BF16),
            pltpu.VMEM((CLASSES, PEOPLE), BF16),
            pltpu.VMEM((CLASSES, PEOPLE), BF16),
            pltpu.VMEM((LANES, PEOPLE), BF16),
            pltpu.VMEM((STACK, 8, LANES), F32),
            pltpu.VMEM((8, LANES), F32),
            pltpu.VMEM((STACK, 8, LANES), F32),
            pltpu.VMEM((ROWS, CLASSES, SIDE), BF16),
            pltpu.VMEM((3, ROWS, 128, SIDE), BF16),
            pltpu.VMEM((ROWS, 128, SIDE), F32),
            pltpu.VMEM((3, ROWS, CLS_LOC, SIDE), F32),
            pltpu.VMEM((CLASSES, 2 * LANES), F32),
            pltpu.VMEM((3, 128, 2 * LANES), F32),
            pltpu.VMEM((128, 2 * LANES), F32),
            pltpu.VMEM((3, CLS_LOC, 2 * LANES), F32),
            dma((3,)), dma((2,)), dma((NCHUNK,)),
            dma((n,)), dma((n,)), dma((n,)), dma((n,)),
            dma((BATCHES, n)), dma((BATCHES, n)), dma((NCHUNK, n)), dma((NCHUNK, n)),
            dma((NCHUNK, 2, 3)), dma((NCHUNK, 2, 3)), dma((NCHUNK, 2, 3)), dma((NCHUNK, 2, 3)),
            dma((2, 3)), dma((2, 3)),
        ],
        compiler_params=pltpu.CompilerParams(
            collective_id=0, has_side_effects=True, vmem_limit_bytes=63 * 1024 * 1024
        ),
        name="class_sums",
    )(angles, groups, chances.reshape(-1), tile, particles, left_maps, right_maps, ctf_table)
    return (jnp.transpose(sums, (1, 0, 2)), jnp.transpose(weights, (1, 0, 2)), norms[:, 0])


def solution(mesh):
    return jax.shard_map(
        per_device,
        mesh=mesh,
        in_specs=(
            P(("stack", "cls"), None, None),
            P(("stack", "cls")),
            P(("stack", "cls")),
            P(("stack", "cls")),
            P(("stack", "cls"), None),
            P(),
            P(),
            P(),
        ),
        out_specs=(P("cls", "stack", None), P("cls", "stack", None), P("cls")),
        check_vma=False,
    )
```

```python
import jax
import jax.numpy as jnp
from jax import lax
from jax.experimental import pallas as pl
from jax.experimental.pallas import tpu as pltpu
from jax.sharding import PartitionSpec as P

MESH = pl.DeviceIdType.MESH
F32 = jnp.float32
BF16 = jnp.bfloat16
SIDE = 256
ANGLES = 16
GROUPS = 16
LOCAL = 64
BATCH = 16
BATCHES = LOCAL // BATCH
STACK = 8
OWNERS = 16
CLS_LOC = 32
CLASSES = OWNERS * CLS_LOC
ROWS = SIDE // STACK
PEOPLE = STACK * LOCAL
PITCH = SIDE + 8
TOGETHER = 8
LANES = 128
CHUNKS = (6, 6, 4, 4, 4, 4, 2, 2)
STARTS = tuple(sum(CHUNKS[:n]) for n in range(len(CHUNKS)))
NCHUNK = len(CHUNKS)
AHEAD = 2
FIRST_LAG = 1
SECOND_LAG = 2
STACK_STEPS = tuple((dy, dc) for dy in (2, 1, 3, 0) for dc in (0, 1) if (dy, dc) != (0, 0))
NT = (((1,), (1,)), ((), ()))


def body(
    angles, groups, class_row, group_row, chance_rows, particles, left_hbm, right_hbm, ctf_hbm,
    sums_out, weights_out, norms_out,
    left, right, ctf, images, weighted, power, outgoing, gathered,
    hot_a, hot_b, mixed, tile, posterior, tiles, norm_tile, norm_tiles,
    partial, first_in, second, second_in,
    small, small_first, small_mid, small_second, staged,
    load_sem, image_sem, own_sem,
    tile_send, tile_recv, norm_send, norm_recv,
    early_send, early_recv, y_send, y_recv,
    first_send, first_recv, second_send, second_recv,
    small_send, small_recv, result_sem,
):
    s = lax.axis_index("stack")
    k = lax.axis_index("cls")
    y, core = s // 2, s % 2
    z, x = k // 4, k % 4

    def along_stack(step):
        return (((y + step[0]) % 4) * 2 + (core + step[1]) % 2, k)

    def along_x(d):
        return (s, z * 4 + (x + d) % 4)

    def along_z(d):
        return (s, ((z + d) % 4) * 4 + x)

    loads = [
        pltpu.make_async_copy(left_hbm, left, load_sem.at[0]),
        pltpu.make_async_copy(right_hbm, right, load_sem.at[1]),
        pltpu.make_async_copy(ctf_hbm, ctf, load_sem.at[2]),
    ]

    def image_load(b):
        return pltpu.make_async_copy(
            particles.at[pl.ds(b * BATCH, BATCH)], images.at[b % 2], image_sem.at[b % 2]
        )

    loads[1].start()
    image_load(0).start()
    loads[0].start()
    loads[2].start()
    image_load(1).start()

    labels = jnp.concatenate(
        [class_row[...].astype(F32), group_row[...].astype(F32), chance_rows[...].astype(F32)], axis=0
    )
    tile[0:4, :] = jnp.concatenate([labels, labels], axis=1)
    tile[4:8, :] = jnp.zeros((4, LANES), F32)
    to_scalars = pltpu.make_async_copy(tile, posterior, load_sem.at[3])
    to_scalars.start()

    barrier = pltpu.get_barrier_semaphore()
    peers = [along_stack(step) for step in STACK_STEPS]
    peers += [along_x(d) for d in (1, 2, 3)] + [along_z(d) for d in (1, 2, 3)]
    for peer in peers:
        pl.semaphore_signal(barrier, inc=1, device_id=peer, device_id_type=MESH)

    def remote(src, dst, send, recv, peer):
        return pltpu.make_async_remote_copy(
            src_ref=src, dst_ref=dst, send_sem=send, recv_sem=recv, device_id=peer, device_id_type=MESH
        )

    def tile_copies():
        return [
            remote(tile, tiles.at[s], tile_send.at[n], tile_recv.at[n], along_stack(step))
            for n, step in enumerate(STACK_STEPS)
        ]

    def norm_copies():
        return [
            remote(norm_tile, norm_tiles.at[s], norm_send.at[n], norm_recv.at[n], along_stack(step))
            for n, step in enumerate(STACK_STEPS)
        ]

    def early_copies(b):
        rows = CHUNKS[0]
        out = []
        for n, step in enumerate(STACK_STEPS):
            peer = along_stack(step)
            out.append(
                remote(
                    outgoing.at[pl.ds(peer[0] * ROWS, rows), pl.ds(b * BATCH, BATCH)],
                    gathered.at[s, pl.ds(0, rows), pl.ds(b * BATCH, BATCH)],
                    early_send.at[b, n], early_recv.at[b, n], peer,
                )
            )
        return out

    def y_copies(c):
        start, rows = STARTS[c], CHUNKS[c]
        out = []
        for n, step in enumerate(STACK_STEPS):
            peer = along_stack(step)
            out.append(
                remote(
                    outgoing.at[pl.ds(peer[0] * ROWS + start, rows)],
                    gathered.at[s, pl.ds(start, rows)],
                    y_send.at[c, n], y_recv.at[c, n], peer,
                )
            )
        return out

    def own_copy(c):
        start, rows = STARTS[c], CHUNKS[c]
        return pltpu.make_async_copy(
            outgoing.at[pl.ds(s * ROWS + start, rows)],
            gathered.at[s, pl.ds(start, rows)],
            own_sem.at[c],
        )

    def first_copies(c):
        half = CHUNKS[c] // 2
        out = []
        for d in (1, 2, 3):
            for part, (hop, spot) in enumerate(((along_x, (x + d) % 4), (along_z, (z + d) % 4))):
                rows = pl.ds(STARTS[c] + part * half, half)
                out.append(
                    remote(
                        partial.at[spot, rows], first_in.at[d - 1, rows],
                        first_send.at[c, part, d - 1], first_recv.at[c, part, d - 1], hop(d),
                    )
                )
        return out

    def second_copies(c):
        half = CHUNKS[c] // 2
        out = []
        for d in (1, 2, 3):
            for part, (hop, spot) in enumerate(((along_z, (z + d) % 4), (along_x, (x + d) % 4))):
                rows = pl.ds(STARTS[c] + part * half, half)
                out.append(
                    remote(
                        second.at[spot, rows], second_in.at[d - 1, rows],
                        second_send.at[c, part, d - 1], second_recv.at[c, part, d - 1], hop(d),
                    )
                )
        return out

    def small_first_copies():
        return [
            remote(
                small.at[pl.ds(((x + d) % 4) * 128, 128)], small_first.at[d - 1],
                small_send.at[0, d - 1], small_recv.at[0, d - 1], along_x(d),
            )
            for d in (1, 2, 3)
        ]

    def small_second_copies():
        return [
            remote(
                small_mid.at[pl.ds(((z + d) % 4) * CLS_LOC, CLS_LOC)], small_second.at[d - 1],
                small_send.at[1, d - 1], small_recv.at[1, d - 1], along_z(d),
            )
            for d in (1, 2, 3)
        ]

    def start(copies):
        for copy in copies:
            copy.start()

    def arrive(copies):
        for copy in copies:
            copy.wait_recv()

    def leave(copies):
        for copy in copies:
            copy.wait_send()

    for b in range(BATCHES):
        if b == 0:
            loads[1].wait()
        image_load(b).wait()
        if b == 0:
            loads[0].wait()
            loads[2].wait()
            to_scalars.wait()

        def several(n, carry, b=b):
            spots = [n * TOGETHER + m for m in range(TOGETHER)]
            turns, sheared = [], []
            for i in spots:
                turn = angles[b * BATCH + i]
                turns.append((turn, (turn + 1) & (ANGLES - 1)))
            for i, near in zip(spots, turns):
                image = images[b % 2, i]
                sheared.append([
                    lax.dot_general(image, right[turn], NT, preferred_element_type=F32).astype(BF16)
                    for turn in near
                ])
            for i, near, pair in zip(spots, turns, sheared):
                p = b * BATCH + i
                spun = posterior[2, p] * jnp.dot(left[near[0]], pair[0], preferred_element_type=F32)
                spun += posterior[3, p] * jnp.dot(left[near[1]], pair[1], preferred_element_type=F32)
                spun = ctf[groups[p]] * spun
                weighted[0, pl.ds(i * PITCH, SIDE), :] = spun[:, :LANES]
                weighted[1, pl.ds(i * PITCH, SIDE), :] = spun[:, LANES:]
                squares = jnp.sum(spun * spun, axis=0, keepdims=True)
                power[pl.ds(p, 1), :] = squares[:, :LANES] + squares[:, LANES:]
            return carry

        lax.fori_loop(0, BATCH // TOGETHER, several, 0)
        if b + 2 < BATCHES:
            image_load(b + 2).start()

        def turn_over(r, carry, b=b):
            for h in range(2):
                lines = weighted[h, pl.ds(r, BATCH, stride=PITCH), :]
                outgoing[r, b * BATCH:(b + 1) * BATCH, h * LANES:(h + 1) * LANES] = lines.astype(BF16)
            return carry

        lax.fori_loop(0, SIDE, turn_over, 0, unroll=8)
        if b == 0:
            pl.semaphore_wait(barrier, len(peers))
            start(tile_copies())
        start(early_copies(b))

    for c in range(1, AHEAD):
        start(y_copies(c))
    for c in range(NCHUNK):
        own_copy(c).start()

    tiles[s] = tile[...]
    lane = lax.broadcasted_iota(jnp.int32, (8, LANES), 1)
    own_power = jnp.sum(power[...], axis=1, keepdims=True) * (1.0 / (SIDE * SIDE))
    spot = lax.broadcasted_iota(jnp.int32, (LOCAL, LANES), 1) & (LOCAL - 1)
    line = lax.broadcasted_iota(jnp.int32, (LOCAL, LANES), 0)
    own_power = jnp.sum(jnp.where(spot == line, own_power, 0.0), axis=0, keepdims=True)
    norm_tile[...] = jnp.broadcast_to(own_power, (8, LANES))
    norm_tiles[s] = jnp.broadcast_to(own_power, (8, LANES))
    start(norm_copies())

    arrive(tile_copies())
    q = lax.broadcasted_iota(jnp.int32, (CLASSES, LANES), 0)
    swapped = (((q >> 5) & 3) * 4 + (q >> 7)) * CLS_LOC + (q & (CLS_LOC - 1))
    natural = q.astype(F32)
    swapped = swapped.astype(F32)
    which = lax.broadcasted_iota(jnp.int32, (LANES, LANES), 0)
    which_group = (which & (GROUPS - 1)).astype(F32)
    for j in range(STACK // 2):
        cols = slice(j * LANES, (j + 1) * LANES)
        both = jnp.where(lane < LOCAL, tiles[2 * j], tiles[2 * j + 1])
        hot_a[:, cols] = jnp.where(swapped == both[0:1], 1.0, 0.0).astype(BF16)
        hot_b[:, cols] = jnp.where(natural == both[0:1], 1.0, 0.0).astype(BF16)
        chance = jnp.where(which < GROUPS, both[2:3], both[3:4])
        keep = (which_group == both[1:2]) & (which < 2 * GROUPS)
        mixed[:, cols] = jnp.where(keep, chance, 0.0).astype(BF16)

    def keep_lines(which, r, lines):
        at = pl.ds((which * ROWS + r) * CLS_LOC, CLS_LOC)
        weighted[0, at, :] = lines[:, :LANES]
        weighted[1, at, :] = lines[:, LANES:]

    def result_copy(which, block):
        rows = pl.ds(block * 8, 8)
        target = (sums_out, weights_out)[which]
        return pltpu.make_async_copy(
            staged.at[which, :, rows], target.at[:, rows], result_sem.at[which, block]
        )

    def settle(which, block):
        def one_class(i, carry):
            for h in range(2):
                at = pl.ds((which * ROWS + block * 8) * CLS_LOC + i, 8, stride=CLS_LOC)
                staged[which, i, block * 8:block * 8 + 8, h * LANES:(h + 1) * LANES] = weighted[h, at, :]
            return carry

        lax.fori_loop(0, CLS_LOC, one_class, 0, unroll=8)
        result_copy(which, block).start()

    def small_start():
        arrive(norm_copies())
        total = jnp.zeros((CLASSES, LANES), F32)
        for j in range(STACK // 2):
            both = jnp.where(lane < LOCAL, tiles[2 * j], tiles[2 * j + 1])
            norm = jnp.where(lane < LOCAL, norm_tiles[2 * j], norm_tiles[2 * j + 1])
            total += jnp.where(swapped == both[0:1], norm[0:1], 0.0)
        small[:, 0:LANES] = total
        small[:, LANES:2 * LANES] = lax.dot_general(hot_a[...], mixed[...], NT, preferred_element_type=F32)
        start(small_first_copies())

    def small_middle():
        arrive(small_first_copies())
        small_mid[...] = (
            small[pl.ds(x * 128, 128), :] + small_first[0] + small_first[1] + small_first[2]
        )
        start(small_second_copies())

    def small_end():
        arrive(small_second_copies())
        total = small_mid[pl.ds(z * CLS_LOC, CLS_LOC), :] + small_second[0] + small_second[1] + small_second[2]
        norms = jnp.sum(total[:, :LANES], axis=1, keepdims=True)
        norms_out[...] = jnp.broadcast_to(norms, (CLS_LOC, LANES))
        coef = total[:, LANES:LANES + GROUPS] + total[:, LANES + GROUPS:LANES + 2 * GROUPS]

        def weigh(r, carry):
            lines = jnp.concatenate([ctf[g, pl.ds(s * ROWS + r, 1), :] for g in range(GROUPS)], axis=0)
            spread = jnp.dot(
                coef, lines * lines, precision=lax.Precision.HIGHEST, preferred_element_type=F32
            )
            keep_lines(1, r, spread)
            return carry

        lax.fori_loop(0, ROWS, weigh, 0)
        for block in range(ROWS // 8):
            settle(1, block)

    def by_class(c):
        half = CHUNKS[c] // 2
        for part, hot in enumerate((hot_a, hot_b)):

            def add(i, carry, part=part, hot=hot):
                r = STARTS[c] + part * half + i
                lines = gathered[:, r].reshape(PEOPLE, SIDE)
                sums = jnp.dot(hot[...], lines, preferred_element_type=F32).astype(BF16)
                partial[:, r] = sums.reshape(4, 128, SIDE)
                return carry

            lax.fori_loop(0, half, add, 0)

    def add_first(c):
        half = CHUNKS[c] // 2
        for part, mine in enumerate((x, z)):

            def add(i, carry, part=part, mine=mine):
                r = STARTS[c] + part * half + i
                total = partial[mine, r].astype(F32)
                for d in range(3):
                    total += first_in[d, r].astype(F32)
                second[:, r] = total.reshape(4, CLS_LOC, SIDE)
                return carry

            lax.fori_loop(0, half, add, 0)

    def add_second(c):
        half = CHUNKS[c] // 2
        for part, mine in enumerate((z, x)):

            def add(i, carry, part=part, mine=mine):
                r = STARTS[c] + part * half + i
                total = second[mine, r]
                for d in range(3):
                    total += second_in[d, r]
                keep_lines(0, r, total)
                return carry

            lax.fori_loop(0, half, add, 0)

    for c in range(NCHUNK + SECOND_LAG):
        if c < NCHUNK:
            if c == 0:
                for b in range(BATCHES):
                    arrive(early_copies(b))
            else:
                arrive(y_copies(c))
            if c + AHEAD < NCHUNK:
                start(y_copies(c + AHEAD))
            own_copy(c).wait()
            by_class(c)
            start(first_copies(c))
        if c == 0:
            small_start()
        if c == 1:
            small_middle()
        if 0 <= c - FIRST_LAG < NCHUNK:
            arrive(first_copies(c - FIRST_LAG))
            add_first(c - FIRST_LAG)
            start(second_copies(c - FIRST_LAG))
        if c == 2:
            small_end()
        if 0 <= c - SECOND_LAG < NCHUNK:
            arrive(second_copies(c - SECOND_LAG))
            add_second(c - SECOND_LAG)
            begun = STARTS[c - SECOND_LAG]
            for block in range(begun // 8, (begun + CHUNKS[c - SECOND_LAG]) // 8):
                settle(0, block)

    leave(tile_copies())
    leave(norm_copies())
    for b in range(BATCHES):
        leave(early_copies(b))
    for c in range(NCHUNK):
        if c > 0:
            leave(y_copies(c))
        leave(first_copies(c))
        leave(second_copies(c))
    leave(small_first_copies())
    leave(small_second_copies())
    for which in range(2):
        for block in range(ROWS // 8):
            result_copy(which, block).wait()


def per_device(particles, classes, angles, groups, posterior, left_maps, right_maps, ctf_table):
    smem = pl.BlockSpec(memory_space=pltpu.SMEM)
    vmem = pl.BlockSpec(memory_space=pltpu.VMEM)
    hbm = pl.BlockSpec(memory_space=pl.ANY)
    n = len(STACK_STEPS)
    dma = pltpu.SemaphoreType.DMA
    sums, weights, norms = pl.pallas_call(
        body,
        out_shape=(
            jax.ShapeDtypeStruct((CLS_LOC, ROWS, SIDE), F32),
            jax.ShapeDtypeStruct((CLS_LOC, ROWS, SIDE), F32),
            jax.ShapeDtypeStruct((CLS_LOC, LANES), F32),
        ),
        in_specs=[smem, smem, vmem, vmem, vmem, hbm, hbm, hbm, hbm],
        out_specs=(hbm, hbm, vmem),
        scratch_shapes=[
            pltpu.VMEM((ANGLES, SIDE, SIDE), BF16),
            pltpu.VMEM((ANGLES, SIDE, SIDE), BF16),
            pltpu.VMEM((GROUPS, SIDE, SIDE), F32),
            pltpu.VMEM((2, BATCH, SIDE, SIDE), BF16),
            pltpu.VMEM((2, BATCH * PITCH, LANES), F32),
            pltpu.VMEM((LOCAL, LANES), F32),
            pltpu.VMEM((SIDE, LOCAL, SIDE), BF16),
            pltpu.VMEM((STACK, ROWS, LOCAL, SIDE), BF16),
            pltpu.VMEM((CLASSES, PEOPLE), BF16),
            pltpu.VMEM((CLASSES, PEOPLE), BF16),
            pltpu.VMEM((LANES, PEOPLE), BF16),
            pltpu.VMEM((8, LANES), F32),
            pltpu.SMEM((8, LANES), F32),
            pltpu.VMEM((STACK, 8, LANES), F32),
            pltpu.VMEM((8, LANES), F32),
            pltpu.VMEM((STACK, 8, LANES), F32),
            pltpu.VMEM((4, ROWS, 128, SIDE), BF16),
            pltpu.VMEM((3, ROWS, 128, SIDE), BF16),
            pltpu.VMEM((4, ROWS, CLS_LOC, SIDE), F32),
            pltpu.VMEM((3, ROWS, CLS_LOC, SIDE), F32),
            pltpu.VMEM((CLASSES, 2 * LANES), F32),
            pltpu.VMEM((3, 128, 2 * LANES), F32),
            pltpu.VMEM((128, 2 * LANES), F32),
            pltpu.VMEM((3, CLS_LOC, 2 * LANES), F32),
            pltpu.VMEM((2, CLS_LOC, ROWS, SIDE), F32),
            dma((4,)), dma((2,)), dma((NCHUNK,)),
            dma((n,)), dma((n,)), dma((n,)), dma((n,)),
            dma((BATCHES, n)), dma((BATCHES, n)), dma((NCHUNK, n)), dma((NCHUNK, n)),
            dma((NCHUNK, 2, 3)), dma((NCHUNK, 2, 3)), dma((NCHUNK, 2, 3)), dma((NCHUNK, 2, 3)),
            dma((2, 3)), dma((2, 3)), dma((2, ROWS // 8)),
        ],
        compiler_params=pltpu.CompilerParams(
            collective_id=0, has_side_effects=True, vmem_limit_bytes=63 * 1024 * 1024
        ),
        name="class_sums",
    )(angles, groups, classes.reshape(1, LOCAL), groups.reshape(1, LOCAL), posterior.T, particles, left_maps, right_maps, ctf_table)
    return (sums, weights, norms[:, 0])


def solution(mesh):
    return jax.shard_map(
        per_device,
        mesh=mesh,
        in_specs=(
            P(("stack", "cls"), None, None),
            P(("stack", "cls")),
            P(("stack", "cls")),
            P(("stack", "cls")),
            P(("stack", "cls"), None),
            P(),
            P(),
            P(),
        ),
        out_specs=(P("cls", "stack", None), P("cls", "stack", None), P("cls")),
        check_vma=False,
    )
```

```python
import jax
import jax.numpy as jnp
from jax import lax
from jax.experimental import pallas as pl
from jax.experimental.pallas import tpu as pltpu
from jax.sharding import PartitionSpec as P

MESH = pl.DeviceIdType.MESH
F32 = jnp.float32
BF16 = jnp.bfloat16
SIDE = 256
ANGLES = 16
GROUPS = 16
LOCAL = 64
BATCH = 16
BATCHES = LOCAL // BATCH
STACK = 8
OWNERS = 16
CLS_LOC = 32
CLASSES = OWNERS * CLS_LOC
ROWS = SIDE // STACK
PEOPLE = STACK * LOCAL
PITCH = SIDE + 8
TOGETHER = 8
LANES = 128
CHUNKS = (4, 4, 4, 4, 4, 2, 2)
SIDEWAYS = 8
SIDES = 2
STRAIGHT = ROWS - SIDEWAYS
STARTS = tuple(SIDEWAYS + sum(CHUNKS[:n]) for n in range(len(CHUNKS)))
NCHUNK = len(CHUNKS)
AHEAD = 2
FIRST_LAG = 1
SECOND_LAG = 2
SIDE_LAGS = (2, 4)
STACK_STEPS = tuple((dy, dc) for dy in (2, 1, 3, 0) for dc in (0, 1) if (dy, dc) != (0, 0))
ACROSS_STEPS = tuple((dx, dc) for dx in (2, 1, 3, 0) for dc in (0, 1) if (dx, dc) != (0, 0))
NT = (((1,), (1,)), ((), ()))


def body(
    angles, groups, class_row, group_row, chance_rows, particles, left_hbm, right_hbm, ctf_hbm,
    sums_out, weights_out, norms_out,
    left, right, ctf, images, weighted, power, outgoing, gathered,
    hot, hot_x, mixed, tile, posterior, tiles, tiles_x, norm_tile, norm_tiles,
    partial, first_in, second, second_in,
    small, small_first, small_mid, small_second, staged, side_second_in, side_third, side_third_in,
    load_sem, image_sem, own_sem,
    tile_send, tile_recv, norm_send, norm_recv,
    early_send, early_recv, y_send, y_recv,
    first_send, first_recv, second_send, second_recv,
    small_send, small_recv, result_sem,
    across_send, across_recv, tile_x_send, tile_x_recv, side_send, side_recv, side_own_sem,
):
    s = lax.axis_index("stack")
    k = lax.axis_index("cls")
    y, core = s // 2, s % 2
    z, x = k // 4, k % 4

    def along_stack(step):
        return (((y + step[0]) % 4) * 2 + (core + step[1]) % 2, k)

    def across(side, step):
        there = (z * 4 + (x + step[0]) % 4, ((z + step[0]) % 4) * 4 + x)[side]
        return (y * 2 + (core + step[1]) % 2, there)

    def along_x(d):
        return (s, z * 4 + (x + d) % 4)

    def along_z(d):
        return (s, ((z + d) % 4) * 4 + x)

    def along_y(d):
        return (((y + d) % 4) * 2 + core, k)

    wide, deep = (x, z), (z, x)
    along_wide, along_deep = (along_x, along_z), (along_z, along_x)

    def spread_at(side):
        return wide[side] * 2 + core


    loads = [
        pltpu.make_async_copy(left_hbm, left, load_sem.at[0]),
        pltpu.make_async_copy(right_hbm, right, load_sem.at[1]),
        pltpu.make_async_copy(ctf_hbm, ctf, load_sem.at[2]),
    ]

    def image_load(b):
        return pltpu.make_async_copy(
            particles.at[pl.ds(b * BATCH, BATCH)], images.at[b % 2], image_sem.at[b % 2]
        )

    loads[1].start()
    image_load(0).start()
    loads[0].start()
    loads[2].start()
    image_load(1).start()

    labels = jnp.concatenate(
        [class_row[...].astype(F32), group_row[...].astype(F32), chance_rows[...].astype(F32)], axis=0
    )
    tile[0:4, :] = jnp.concatenate([labels, labels], axis=1)
    tile[4:8, :] = jnp.zeros((4, LANES), F32)
    to_scalars = pltpu.make_async_copy(tile, posterior, load_sem.at[3])
    to_scalars.start()

    barrier = pltpu.get_barrier_semaphore()
    peers = [along_stack(step) for step in STACK_STEPS]
    for side in range(SIDES):
        peers += [across(side, step) for step in ACROSS_STEPS if step[0] != 0 and step[1] != 0]
    peers += [along_x(d) for d in (1, 2, 3)] + [along_z(d) for d in (1, 2, 3)]
    for peer in peers:
        pl.semaphore_signal(barrier, inc=1, device_id=peer, device_id_type=MESH)

    def remote(src, dst, send, recv, peer):
        return pltpu.make_async_remote_copy(
            src_ref=src, dst_ref=dst, send_sem=send, recv_sem=recv, device_id=peer, device_id_type=MESH
        )

    def tile_copies():
        return [
            remote(tile, tiles.at[s], tile_send.at[n], tile_recv.at[n], along_stack(step))
            for n, step in enumerate(STACK_STEPS)
        ]

    def tile_x_copies():
        return [
            remote(
                tile, tiles_x.at[side, spread_at(side)],
                tile_x_send.at[side, n], tile_x_recv.at[side, n], across(side, step),
            )
            for side in range(SIDES)
            for n, step in enumerate(ACROSS_STEPS)
        ]

    def sideways(side, spot):
        return side * STACK * 4 + spot * 4

    def across_copies(b):
        out = []
        for n, step in enumerate(ACROSS_STEPS):
            for side in range(SIDES):
                spot = ((wide[side] + step[0]) % 4) * 2 + (core + step[1]) % 2
                out.append(
                    remote(
                        outgoing.at[pl.ds(sideways(side, spot), 4), pl.ds(b * BATCH, BATCH)],
                        gathered.at[spread_at(side), pl.ds(side * 4, 4), pl.ds(b * BATCH, BATCH)],
                        across_send.at[b, side, n], across_recv.at[b, side, n], across(side, step),
                    )
                )
        return out

    def across_own(side):
        return pltpu.make_async_copy(
            outgoing.at[pl.ds(sideways(side, spread_at(side)), 4)],
            gathered.at[spread_at(side), pl.ds(side * 4, 4)],
            side_own_sem.at[side],
        )

    def side_first(side):
        rows = pl.ds(side * 4, 4)
        return [
            remote(
                partial.at[(deep[side] + d) % 4, rows], first_in.at[d - 1, rows],
                side_send.at[side, 0, d - 1], side_recv.at[side, 0, d - 1], along_deep[side](d),
            )
            for d in (1, 2, 3)
        ]

    def side_second(side):
        return [
            remote(
                second.at[:, pl.ds(side * 4 + (y + d) % 4, 1)], side_second_in.at[side, d - 1],
                side_send.at[side, 1, d - 1], side_recv.at[side, 1, d - 1], along_y(d),
            )
            for d in (1, 2, 3)
        ]

    def side_last(side):
        return [
            remote(
                side_third.at[side, (wide[side] + d) % 4], side_third_in.at[side, d - 1],
                side_send.at[side, 2, d - 1], side_recv.at[side, 2, d - 1], along_wide[side](d),
            )
            for d in (1, 2, 3)
        ]

    def norm_copies():
        return [
            remote(norm_tile, norm_tiles.at[s], norm_send.at[n], norm_recv.at[n], along_stack(step))
            for n, step in enumerate(STACK_STEPS)
        ]

    def straight(block, row):
        return STACK * SIDEWAYS + block * STRAIGHT + row - SIDEWAYS

    def early_copies(b):
        rows = CHUNKS[0]
        out = []
        for n, step in enumerate(STACK_STEPS):
            peer = along_stack(step)
            out.append(
                remote(
                    outgoing.at[pl.ds(straight(peer[0], STARTS[0]), rows), pl.ds(b * BATCH, BATCH)],
                    gathered.at[s, pl.ds(STARTS[0], rows), pl.ds(b * BATCH, BATCH)],
                    early_send.at[b, n], early_recv.at[b, n], peer,
                )
            )
        return out

    def y_copies(c):
        start, rows = STARTS[c], CHUNKS[c]
        out = []
        for n, step in enumerate(STACK_STEPS):
            peer = along_stack(step)
            out.append(
                remote(
                    outgoing.at[pl.ds(straight(peer[0], start), rows)],
                    gathered.at[s, pl.ds(start, rows)],
                    y_send.at[c, n], y_recv.at[c, n], peer,
                )
            )
        return out

    def own_copy(c):
        start, rows = STARTS[c], CHUNKS[c]
        return pltpu.make_async_copy(
            outgoing.at[pl.ds(straight(s, start), rows)],
            gathered.at[s, pl.ds(start, rows)],
            own_sem.at[c],
        )

    def first_copies(c):
        half = CHUNKS[c] // 2
        out = []
        for d in (1, 2, 3):
            for part, (hop, spot) in enumerate(((along_x, (x + d) % 4), (along_z, (z + d) % 4))):
                rows = pl.ds(STARTS[c] + part * half, half)
                out.append(
                    remote(
                        partial.at[spot, rows], first_in.at[d - 1, rows],
                        first_send.at[c, part, d - 1], first_recv.at[c, part, d - 1], hop(d),
                    )
                )
        return out

    def second_copies(c):
        half = CHUNKS[c] // 2
        out = []
        for d in (1, 2, 3):
            for part, (hop, spot) in enumerate(((along_z, (z + d) % 4), (along_x, (x + d) % 4))):
                rows = pl.ds(STARTS[c] + part * half, half)
                out.append(
                    remote(
                        second.at[spot, rows], second_in.at[d - 1, pl.ds(STARTS[c] - SIDEWAYS + part * half, half)],
                        second_send.at[c, part, d - 1], second_recv.at[c, part, d - 1], hop(d),
                    )
                )
        return out

    def small_first_copies():
        return [
            remote(
                small.at[pl.ds(((x + d) % 4) * 128, 128)], small_first.at[d - 1],
                small_send.at[0, d - 1], small_recv.at[0, d - 1], along_x(d),
            )
            for d in (1, 2, 3)
        ]

    def small_second_copies():
        return [
            remote(
                small_mid.at[pl.ds(((z + d) % 4) * CLS_LOC, CLS_LOC)], small_second.at[d - 1],
                small_send.at[1, d - 1], small_recv.at[1, d - 1], along_z(d),
            )
            for d in (1, 2, 3)
        ]

    def start(copies):
        for copy in copies:
            copy.start()

    def arrive(copies):
        for copy in copies:
            copy.wait_recv()

    def leave(copies):
        for copy in copies:
            copy.wait_send()

    for b in range(BATCHES):
        if b == 0:
            loads[1].wait()
        image_load(b).wait()
        if b == 0:
            loads[0].wait()
            loads[2].wait()
            to_scalars.wait()

        def several(n, carry, b=b):
            spots = [n * TOGETHER + m for m in range(TOGETHER)]
            turns, sheared = [], []
            for i in spots:
                turn = angles[b * BATCH + i]
                turns.append((turn, (turn + 1) & (ANGLES - 1)))
            for i, near in zip(spots, turns):
                image = images[b % 2, i]
                sheared.append([
                    lax.dot_general(image, right[turn], NT, preferred_element_type=F32).astype(BF16)
                    for turn in near
                ])
            for i, near, pair in zip(spots, turns, sheared):
                p = b * BATCH + i
                spun = posterior[2, p] * jnp.dot(left[near[0]], pair[0], preferred_element_type=F32)
                spun += posterior[3, p] * jnp.dot(left[near[1]], pair[1], preferred_element_type=F32)
                spun = ctf[groups[p]] * spun
                weighted[0, pl.ds(i * PITCH, SIDE), :] = spun[:, :LANES]
                weighted[1, pl.ds(i * PITCH, SIDE), :] = spun[:, LANES:]
                squares = jnp.sum(spun * spun, axis=0, keepdims=True)
                power[pl.ds(p, 1), :] = squares[:, :LANES] + squares[:, LANES:]
            return carry

        lax.fori_loop(0, BATCH // TOGETHER, several, 0)
        if b + 2 < BATCHES:
            image_load(b + 2).start()

        def turn_over(block, carry, b=b):
            for r in range(ROWS):
                if r < SIDEWAYS:
                    place = sideways(r // 4, (r % 4) * 2 + (block & 1)) + (block >> 1)
                else:
                    place = straight(block, r)
                for h in range(2):
                    lines = weighted[h, pl.ds(block * ROWS + r, BATCH, stride=PITCH), :]
                    outgoing[place, b * BATCH:(b + 1) * BATCH, h * LANES:(h + 1) * LANES] = lines.astype(BF16)
            return carry

        lax.fori_loop(0, STACK, turn_over, 0)
        if b == 0:
            pl.semaphore_wait(barrier, len(peers))
            start(tile_copies())
            start(tile_x_copies())
        start(across_copies(b))
        start(early_copies(b))

    for c in range(1, AHEAD):
        start(y_copies(c))
    for c in range(NCHUNK):
        own_copy(c).start()

    for side in range(SIDES):
        across_own(side).start()

    tiles[s] = tile[...]
    for side in range(SIDES):
        tiles_x[side, spread_at(side)] = tile[...]
    lane = lax.broadcasted_iota(jnp.int32, (8, LANES), 1)
    own_power = jnp.sum(power[...], axis=1, keepdims=True) * (1.0 / (SIDE * SIDE))
    spot = lax.broadcasted_iota(jnp.int32, (LOCAL, LANES), 1) & (LOCAL - 1)
    line = lax.broadcasted_iota(jnp.int32, (LOCAL, LANES), 0)
    own_power = jnp.sum(jnp.where(spot == line, own_power, 0.0), axis=0, keepdims=True)
    norm_tile[...] = jnp.broadcast_to(own_power, (8, LANES))
    norm_tiles[s] = jnp.broadcast_to(own_power, (8, LANES))
    start(norm_copies())

    arrive(tile_copies())
    arrive(tile_x_copies())
    natural = lax.broadcasted_iota(jnp.int32, (CLASSES, LANES), 0).astype(F32)
    which = lax.broadcasted_iota(jnp.int32, (LANES, LANES), 0)
    which_group = (which & (GROUPS - 1)).astype(F32)
    for j in range(STACK // 2):
        cols = slice(j * LANES, (j + 1) * LANES)
        both = jnp.where(lane < LOCAL, tiles[2 * j], tiles[2 * j + 1])
        hot[:, cols] = jnp.where(natural == both[0:1], 1.0, 0.0).astype(BF16)
        for side in range(SIDES):
            beside = jnp.where(lane < LOCAL, tiles_x[side, 2 * j], tiles_x[side, 2 * j + 1])
            hot_x[side, :, cols] = jnp.where(natural == beside[0:1], 1.0, 0.0).astype(BF16)
        chance = jnp.where(which < GROUPS, both[2:3], both[3:4])
        keep = (which_group == both[1:2]) & (which < 2 * GROUPS)
        mixed[:, cols] = jnp.where(keep, chance, 0.0).astype(BF16)

    def keep_lines(which, r, lines):
        at = pl.ds(pl.multiple_of((which * ROWS + r) * CLS_LOC, CLS_LOC), CLS_LOC)
        weighted[0, at, :] = lines[:, :LANES]
        weighted[1, at, :] = lines[:, LANES:]

    def result_copy(which, block):
        rows = pl.ds(block * 8, 8)
        target = (sums_out, weights_out)[which]
        return pltpu.make_async_copy(
            staged.at[which, :, rows], target.at[:, rows], result_sem.at[which, block]
        )

    def settle(which, block):
        def one_class(i, carry):
            for h in range(2):
                at = pl.ds((which * ROWS + block * 8) * CLS_LOC + i, 8, stride=CLS_LOC)
                staged[which, i, block * 8:block * 8 + 8, h * LANES:(h + 1) * LANES] = weighted[h, at, :]
            return carry

        lax.fori_loop(0, CLS_LOC, one_class, 0, unroll=8)
        result_copy(which, block).start()

    def small_start():
        arrive(norm_copies())
        total = jnp.zeros((CLASSES, LANES), F32)
        for j in range(STACK // 2):
            both = jnp.where(lane < LOCAL, tiles[2 * j], tiles[2 * j + 1])
            norm = jnp.where(lane < LOCAL, norm_tiles[2 * j], norm_tiles[2 * j + 1])
            total += jnp.where(natural == both[0:1], norm[0:1], 0.0)
        blend = lax.dot_general(hot[...], mixed[...], NT, preferred_element_type=F32)
        for owner in range(OWNERS):
            line = ((owner % 4) * 4 + owner // 4) * CLS_LOC
            small[line:line + CLS_LOC, 0:LANES] = total[owner * CLS_LOC:(owner + 1) * CLS_LOC]
            small[line:line + CLS_LOC, LANES:2 * LANES] = blend[owner * CLS_LOC:(owner + 1) * CLS_LOC]
        start(small_first_copies())

    def small_middle():
        arrive(small_first_copies())
        small_mid[...] = (
            small[pl.ds(x * 128, 128), :] + small_first[0] + small_first[1] + small_first[2]
        )
        start(small_second_copies())

    def small_end():
        arrive(small_second_copies())
        total = small_mid[pl.ds(z * CLS_LOC, CLS_LOC), :] + small_second[0] + small_second[1] + small_second[2]
        norms = jnp.sum(total[:, :LANES], axis=1, keepdims=True)
        norms_out[...] = jnp.broadcast_to(norms, (CLS_LOC, LANES))
        coef = total[:, LANES:LANES + GROUPS] + total[:, LANES + GROUPS:LANES + 2 * GROUPS]

        def weigh(r, carry):
            lines = jnp.concatenate([ctf[g, pl.ds(s * ROWS + r, 1), :] for g in range(GROUPS)], axis=0)
            spread = jnp.dot(
                coef, lines * lines, precision=lax.Precision.HIGHEST, preferred_element_type=F32
            )
            keep_lines(1, r, spread)
            return carry

        lax.fori_loop(0, ROWS, weigh, 0)
        for block in range(ROWS // 8):
            settle(1, block)

    def keep_partial(part, r, sums):
        if part == 0:
            for owner in range(OWNERS):
                line = (owner // 4) * CLS_LOC
                block = sums[owner * CLS_LOC:(owner + 1) * CLS_LOC]
                partial[owner % 4, r, line:line + CLS_LOC, :] = block
        else:
            partial[:, r] = sums.reshape(4, 128, SIDE)

    def by_class(c):
        half = CHUNKS[c] // 2
        for part in range(2):

            def add(i, carry, part=part):
                r = STARTS[c] + part * half + i
                lines = gathered[:, r].reshape(PEOPLE, SIDE)
                sums = jnp.dot(hot[...], lines, preferred_element_type=F32).astype(BF16)
                keep_partial(part, r, sums)
                return carry

            lax.fori_loop(0, half, add, 0)

    def add_first(c):
        half = CHUNKS[c] // 2
        for part, mine in enumerate((x, z)):

            def add(i, carry, part=part, mine=mine):
                r = STARTS[c] + part * half + i
                total = partial[mine, r].astype(F32)
                for d in range(3):
                    total += first_in[d, r].astype(F32)
                second[:, r] = total.reshape(4, CLS_LOC, SIDE)
                return carry

            lax.fori_loop(0, half, add, 0)

    def add_second(c):
        half = CHUNKS[c] // 2
        for part, mine in enumerate((z, x)):

            def add(i, carry, part=part, mine=mine):
                r = STARTS[c] + part * half + i
                total = second[mine, r]
                for d in range(3):
                    total += second_in[d, r - SIDEWAYS]
                keep_lines(0, r, total)
                return carry

            lax.fori_loop(0, half, add, 0)

    def side_by_class(side):
        def add(i, carry):
            r = side * 4 + i
            lines = gathered[:, r].reshape(PEOPLE, SIDE)
            sums = jnp.dot(hot_x[side], lines, preferred_element_type=F32).astype(BF16)
            keep_partial(1 - side, r, sums)
            return carry

        lax.fori_loop(0, 4, add, 0)

    def side_add_first(side):
        def add(i, carry):
            r = side * 4 + i
            total = partial[deep[side], r].astype(F32)
            for d in range(3):
                total += first_in[d, r].astype(F32)
            second[:, r] = total.reshape(4, CLS_LOC, SIDE)
            return carry

        lax.fori_loop(0, 4, add, 0)

    def side_add_second(side):
        for block in range(4):
            total = second[block, side * 4 + y]
            for d in range(3):
                total += side_second_in[side, d, block, 0]
            side_third[side, block] = total

    def side_keep(side):
        keep_lines(0, side * 4 + wide[side], side_third[side, wide[side]])
        for d in (1, 2, 3):
            keep_lines(0, side * 4 + (wide[side] + 4 - d) % 4, side_third_in[side, d - 1])

    for c in range(NCHUNK + SECOND_LAG):
        if c < NCHUNK:
            if c == 0:
                for b in range(BATCHES):
                    arrive(early_copies(b))
            else:
                arrive(y_copies(c))
            if c + AHEAD < NCHUNK:
                start(y_copies(c + AHEAD))
            own_copy(c).wait()
            by_class(c)
            start(first_copies(c))
        if c == 0:
            for b in range(BATCHES):
                arrive(across_copies(b))
            for side in range(SIDES):
                across_own(side).wait()
                side_by_class(side)
                start(side_first(side))
        if c == SIDE_LAGS[0]:
            for side in range(SIDES):
                arrive(side_first(side))
                side_add_first(side)
                start(side_second(side))
        if c == SIDE_LAGS[1]:
            for side in range(SIDES):
                arrive(side_second(side))
                side_add_second(side)
                start(side_last(side))
        if c == NCHUNK:
            for side in range(SIDES):
                arrive(side_last(side))
                side_keep(side)
            settle(0, 0)
        if c == 0:
            small_start()
        if c == 1:
            small_middle()
        if 0 <= c - FIRST_LAG < NCHUNK:
            arrive(first_copies(c - FIRST_LAG))
            add_first(c - FIRST_LAG)
            start(second_copies(c - FIRST_LAG))
        if c == 2:
            small_end()
        if 0 <= c - SECOND_LAG < NCHUNK:
            arrive(second_copies(c - SECOND_LAG))
            add_second(c - SECOND_LAG)
            begun = STARTS[c - SECOND_LAG]
            for block in range(begun // 8, (begun + CHUNKS[c - SECOND_LAG]) // 8):
                settle(0, block)

    leave(tile_copies())
    leave(norm_copies())
    for b in range(BATCHES):
        leave(early_copies(b))
    for c in range(NCHUNK):
        if c > 0:
            leave(y_copies(c))
        leave(first_copies(c))
        leave(second_copies(c))
    leave(small_first_copies())
    leave(small_second_copies())
    leave(tile_x_copies())
    for b in range(BATCHES):
        leave(across_copies(b))
    for side in range(SIDES):
        leave(side_first(side))
        leave(side_second(side))
        leave(side_last(side))
    for which in range(2):
        for block in range(ROWS // 8):
            result_copy(which, block).wait()


def per_device(particles, classes, angles, groups, posterior, left_maps, right_maps, ctf_table):
    smem = pl.BlockSpec(memory_space=pltpu.SMEM)
    vmem = pl.BlockSpec(memory_space=pltpu.VMEM)
    hbm = pl.BlockSpec(memory_space=pl.ANY)
    n = len(STACK_STEPS)
    dma = pltpu.SemaphoreType.DMA
    sums, weights, norms = pl.pallas_call(
        body,
        out_shape=(
            jax.ShapeDtypeStruct((CLS_LOC, ROWS, SIDE), F32),
            jax.ShapeDtypeStruct((CLS_LOC, ROWS, SIDE), F32),
            jax.ShapeDtypeStruct((CLS_LOC, LANES), F32),
        ),
        in_specs=[smem, smem, vmem, vmem, vmem, hbm, hbm, hbm, hbm],
        out_specs=(hbm, hbm, vmem),
        scratch_shapes=[
            pltpu.VMEM((ANGLES, SIDE, SIDE), BF16),
            pltpu.VMEM((ANGLES, SIDE, SIDE), BF16),
            pltpu.VMEM((GROUPS, SIDE, SIDE), F32),
            pltpu.VMEM((2, BATCH, SIDE, SIDE), BF16),
            pltpu.VMEM((2, BATCH * PITCH, LANES), F32),
            pltpu.VMEM((LOCAL, LANES), F32),
            pltpu.VMEM((SIDE, LOCAL, SIDE), BF16),
            pltpu.VMEM((STACK, ROWS, LOCAL, SIDE), BF16),
            pltpu.VMEM((CLASSES, PEOPLE), BF16),
            pltpu.VMEM((SIDES, CLASSES, PEOPLE), BF16),
            pltpu.VMEM((LANES, PEOPLE), BF16),
            pltpu.VMEM((8, LANES), F32),
            pltpu.SMEM((8, LANES), F32),
            pltpu.VMEM((STACK, 8, LANES), F32),
            pltpu.VMEM((SIDES, STACK, 8, LANES), F32),
            pltpu.VMEM((8, LANES), F32),
            pltpu.VMEM((STACK, 8, LANES), F32),
            pltpu.VMEM((4, ROWS, 128, SIDE), BF16),
            pltpu.VMEM((3, ROWS, 128, SIDE), BF16),
            pltpu.VMEM((4, ROWS, CLS_LOC, SIDE), F32),
            pltpu.VMEM((3, STRAIGHT, CLS_LOC, SIDE), F32),
            pltpu.VMEM((CLASSES, 2 * LANES), F32),
            pltpu.VMEM((3, 128, 2 * LANES), F32),
            pltpu.VMEM((128, 2 * LANES), F32),
            pltpu.VMEM((3, CLS_LOC, 2 * LANES), F32),
            pltpu.VMEM((2, CLS_LOC, ROWS, SIDE), F32),
            pltpu.VMEM((SIDES, 3, 4, 1, CLS_LOC, SIDE), F32),
            pltpu.VMEM((SIDES, 4, CLS_LOC, SIDE), F32),
            pltpu.VMEM((SIDES, 3, CLS_LOC, SIDE), F32),
            dma((4,)), dma((2,)), dma((NCHUNK,)),
            dma((n,)), dma((n,)), dma((n,)), dma((n,)),
            dma((BATCHES, n)), dma((BATCHES, n)), dma((NCHUNK, n)), dma((NCHUNK, n)),
            dma((NCHUNK, 2, 3)), dma((NCHUNK, 2, 3)), dma((NCHUNK, 2, 3)), dma((NCHUNK, 2, 3)),
            dma((2, 3)), dma((2, 3)), dma((2, ROWS // 8)),
            dma((BATCHES, SIDES, n)), dma((BATCHES, SIDES, n)), dma((SIDES, n)), dma((SIDES, n)),
            dma((SIDES, 3, 3)), dma((SIDES, 3, 3)), dma((SIDES,)),
        ],
        compiler_params=pltpu.CompilerParams(
            collective_id=0, has_side_effects=True, vmem_limit_bytes=63 * 1024 * 1024
        ),
        name="class_sums",
    )(angles, groups, classes.reshape(1, LOCAL), groups.reshape(1, LOCAL), posterior.T, particles, left_maps, right_maps, ctf_table)
    return (sums, weights, norms[:, 0])


def solution(mesh):
    return jax.shard_map(
        per_device,
        mesh=mesh,
        in_specs=(
            P(("stack", "cls"), None, None),
            P(("stack", "cls")),
            P(("stack", "cls")),
            P(("stack", "cls")),
            P(("stack", "cls"), None),
            P(),
            P(),
            P(),
        ),
        out_specs=(P("cls", "stack", None), P("cls", "stack", None), P("cls")),
        check_vma=False,
    )
```

```python
import jax
import jax.numpy as jnp
from jax import lax
from jax.experimental import pallas as pl
from jax.experimental.pallas import tpu as pltpu
from jax.sharding import PartitionSpec as P

MESH = pl.DeviceIdType.MESH
F32 = jnp.float32
BF16 = jnp.bfloat16
SIDE = 256
ANGLES = 16
GROUPS = 16
LOCAL = 64
BATCH = 16
BATCHES = LOCAL // BATCH
STACK = 8
OWNERS = 16
CLS_LOC = 32
CLASSES = OWNERS * CLS_LOC
ROWS = SIDE // STACK
PEOPLE = STACK * LOCAL
PITCH = SIDE + 8
TOGETHER = 8
PIECES = 4
LANES = 128
CHUNKS = (4, 4, 4, 4, 4, 2, 2)
SIDEWAYS = 8
SIDES = 2
STRAIGHT = ROWS - SIDEWAYS
STARTS = tuple(SIDEWAYS + sum(CHUNKS[:n]) for n in range(len(CHUNKS)))
NCHUNK = len(CHUNKS)
AHEAD = 2
FIRST_LAG = 1
SECOND_LAG = 2
SIDE_LAGS = (2, 4)
STACK_STEPS = tuple((dy, dc) for dy in (2, 1, 3, 0) for dc in (0, 1) if (dy, dc) != (0, 0))
ACROSS_STEPS = tuple((dx, dc) for dx in (2, 1, 3, 0) for dc in (0, 1) if (dx, dc) != (0, 0))
NT = (((1,), (1,)), ((), ()))


def body(
    angles, groups, class_row, group_row, chance_rows, particles, left_hbm, right_hbm, ctf_hbm,
    sums_out, weights_out, norms_out,
    left, right, ctf, images, weighted, power, outgoing, gathered,
    hot, hot_x, mixed, tile, posterior, tiles, tiles_x, norm_tile, norm_tiles,
    partial, first_in, second, second_in,
    small, small_first, small_mid, small_second, staged, side_second_in, side_third, side_third_in,
    load_sem, image_sem, own_sem,
    tile_send, tile_recv, norm_send, norm_recv,
    early_send, early_recv, y_send, y_recv,
    first_send, first_recv, second_send, second_recv,
    small_send, small_recv, result_sem,
    across_send, across_recv, tile_x_send, tile_x_recv, side_send, side_recv, side_own_sem,
):
    s = lax.axis_index("stack")
    k = lax.axis_index("cls")
    y, core = s // 2, s % 2
    z, x = k // 4, k % 4

    def along_stack(step):
        return (((y + step[0]) % 4) * 2 + (core + step[1]) % 2, k)

    def across(side, step):
        there = (z * 4 + (x + step[0]) % 4, ((z + step[0]) % 4) * 4 + x)[side]
        return (y * 2 + (core + step[1]) % 2, there)

    def along_x(d):
        return (s, z * 4 + (x + d) % 4)

    def along_z(d):
        return (s, ((z + d) % 4) * 4 + x)

    def along_y(d):
        return (((y + d) % 4) * 2 + core, k)

    wide, deep = (x, z), (z, x)
    along_wide, along_deep = (along_x, along_z), (along_z, along_x)

    def spread_at(side):
        return wide[side] * 2 + core


    loads = [
        pltpu.make_async_copy(left_hbm, left, load_sem.at[0]),
        pltpu.make_async_copy(right_hbm, right, load_sem.at[1]),
        pltpu.make_async_copy(ctf_hbm, ctf, load_sem.at[2]),
    ]

    def image_load(b):
        return pltpu.make_async_copy(
            particles.at[pl.ds(b * BATCH, BATCH)], images.at[b % 2], image_sem.at[b % 2]
        )

    loads[1].start()
    image_load(0).start()
    loads[0].start()
    loads[2].start()
    image_load(1).start()

    labels = jnp.concatenate(
        [class_row[...].astype(F32), group_row[...].astype(F32), chance_rows[...].astype(F32)], axis=0
    )
    tile[0:4, :] = jnp.concatenate([labels, labels], axis=1)
    tile[4:8, :] = jnp.zeros((4, LANES), F32)
    to_scalars = pltpu.make_async_copy(tile, posterior, load_sem.at[3])
    to_scalars.start()

    barrier = pltpu.get_barrier_semaphore()
    peers = [along_stack(step) for step in STACK_STEPS]
    for side in range(SIDES):
        peers += [across(side, step) for step in ACROSS_STEPS if step[0] != 0 and step[1] != 0]
    peers += [along_x(d) for d in (1, 2, 3)] + [along_z(d) for d in (1, 2, 3)]
    for peer in peers:
        pl.semaphore_signal(barrier, inc=1, device_id=peer, device_id_type=MESH)

    def remote(src, dst, send, recv, peer):
        return pltpu.make_async_remote_copy(
            src_ref=src, dst_ref=dst, send_sem=send, recv_sem=recv, device_id=peer, device_id_type=MESH
        )

    def tile_copies():
        return [
            remote(tile, tiles.at[s], tile_send.at[n], tile_recv.at[n], along_stack(step))
            for n, step in enumerate(STACK_STEPS)
        ]

    def tile_x_copies():
        return [
            remote(
                tile, tiles_x.at[side, spread_at(side)],
                tile_x_send.at[side, n], tile_x_recv.at[side, n], across(side, step),
            )
            for side in range(SIDES)
            for n, step in enumerate(ACROSS_STEPS)
        ]

    def sideways(side, spot):
        return side * STACK * 4 + spot * 4

    def across_copies(b):
        out = []
        for n, step in enumerate(ACROSS_STEPS):
            for side in range(SIDES):
                spot = ((wide[side] + step[0]) % 4) * 2 + (core + step[1]) % 2
                out.append(
                    remote(
                        outgoing.at[pl.ds(sideways(side, spot), 4), pl.ds(b * BATCH, BATCH)],
                        gathered.at[spread_at(side), pl.ds(side * 4, 4), pl.ds(b * BATCH, BATCH)],
                        across_send.at[b, side, n], across_recv.at[b, side, n], across(side, step),
                    )
                )
        return out

    def across_own(side):
        return pltpu.make_async_copy(
            outgoing.at[pl.ds(sideways(side, spread_at(side)), 4)],
            gathered.at[spread_at(side), pl.ds(side * 4, 4)],
            side_own_sem.at[side],
        )

    def side_first(side):
        rows = pl.ds(side * 4, 4)
        return [
            remote(
                partial.at[(deep[side] + d) % 4, rows], first_in.at[d - 1, rows],
                side_send.at[side, 0, d - 1], side_recv.at[side, 0, d - 1], along_deep[side](d),
            )
            for d in (1, 2, 3)
        ]

    def side_second(side):
        return [
            remote(
                second.at[:, pl.ds(side * 4 + (y + d) % 4, 1)], side_second_in.at[side, d - 1],
                side_send.at[side, 1, d - 1], side_recv.at[side, 1, d - 1], along_y(d),
            )
            for d in (1, 2, 3)
        ]

    def side_last(side):
        return [
            remote(
                side_third.at[side, (wide[side] + d) % 4], side_third_in.at[side, d - 1],
                side_send.at[side, 2, d - 1], side_recv.at[side, 2, d - 1], along_wide[side](d),
            )
            for d in (1, 2, 3)
        ]

    def norm_copies():
        return [
            remote(norm_tile, norm_tiles.at[s], norm_send.at[n], norm_recv.at[n], along_stack(step))
            for n, step in enumerate(STACK_STEPS)
        ]

    def straight(block, row):
        return STACK * SIDEWAYS + block * STRAIGHT + row - SIDEWAYS

    def early_copies(b):
        rows = CHUNKS[0]
        out = []
        for n, step in enumerate(STACK_STEPS):
            peer = along_stack(step)
            out.append(
                remote(
                    outgoing.at[pl.ds(straight(peer[0], STARTS[0]), rows), pl.ds(b * BATCH, BATCH)],
                    gathered.at[s, pl.ds(STARTS[0], rows), pl.ds(b * BATCH, BATCH)],
                    early_send.at[b, n], early_recv.at[b, n], peer,
                )
            )
        return out

    def y_copies(c):
        start, rows = STARTS[c], CHUNKS[c]
        out = []
        for n, step in enumerate(STACK_STEPS):
            peer = along_stack(step)
            out.append(
                remote(
                    outgoing.at[pl.ds(straight(peer[0], start), rows)],
                    gathered.at[s, pl.ds(start, rows)],
                    y_send.at[c, n], y_recv.at[c, n], peer,
                )
            )
        return out

    def own_copy(c):
        start, rows = STARTS[c], CHUNKS[c]
        return pltpu.make_async_copy(
            outgoing.at[pl.ds(straight(s, start), rows)],
            gathered.at[s, pl.ds(start, rows)],
            own_sem.at[c],
        )

    def first_copies(c):
        half = CHUNKS[c] // 2
        out = []
        for d in (1, 2, 3):
            for part, (hop, spot) in enumerate(((along_x, (x + d) % 4), (along_z, (z + d) % 4))):
                rows = pl.ds(STARTS[c] + part * half, half)
                out.append(
                    remote(
                        partial.at[spot, rows], first_in.at[d - 1, rows],
                        first_send.at[c, part, d - 1], first_recv.at[c, part, d - 1], hop(d),
                    )
                )
        return out

    def second_copies(c):
        half = CHUNKS[c] // 2
        out = []
        for d in (1, 2, 3):
            for part, (hop, spot) in enumerate(((along_z, (z + d) % 4), (along_x, (x + d) % 4))):
                rows = pl.ds(STARTS[c] + part * half, half)
                out.append(
                    remote(
                        second.at[spot, rows], second_in.at[d - 1, pl.ds(STARTS[c] - SIDEWAYS + part * half, half)],
                        second_send.at[c, part, d - 1], second_recv.at[c, part, d - 1], hop(d),
                    )
                )
        return out

    def small_first_copies():
        return [
            remote(
                small.at[pl.ds(((x + d) % 4) * 128, 128)], small_first.at[d - 1],
                small_send.at[0, d - 1], small_recv.at[0, d - 1], along_x(d),
            )
            for d in (1, 2, 3)
        ]

    def small_second_copies():
        return [
            remote(
                small_mid.at[pl.ds(((z + d) % 4) * CLS_LOC, CLS_LOC)], small_second.at[d - 1],
                small_send.at[1, d - 1], small_recv.at[1, d - 1], along_z(d),
            )
            for d in (1, 2, 3)
        ]

    def start(copies):
        for copy in copies:
            copy.start()

    def arrive(copies):
        for copy in copies:
            copy.wait_recv()

    def leave(copies):
        for copy in copies:
            copy.wait_send()

    for b in range(BATCHES):
        if b == 0:
            loads[1].wait()
        image_load(b).wait()
        if b == 0:
            loads[0].wait()
            loads[2].wait()
            to_scalars.wait()

        def several(n, carry, b=b):
            spots = [n * TOGETHER + m for m in range(TOGETHER)]
            turns, sheared = [], []
            for i in spots:
                turn = angles[b * BATCH + i]
                turns.append((turn, (turn + 1) & (ANGLES - 1)))
            for i, near in zip(spots, turns):
                image = images[b % 2, i]
                sheared.append([
                    lax.dot_general(image, right[turn], NT, preferred_element_type=F32).astype(BF16)
                    for turn in near
                ])
            for i, near, pair in zip(spots, turns, sheared):
                p = b * BATCH + i
                spun = posterior[2, p] * jnp.dot(left[near[0]], pair[0], preferred_element_type=F32)
                spun += posterior[3, p] * jnp.dot(left[near[1]], pair[1], preferred_element_type=F32)
                spun = ctf[groups[p]] * spun
                weighted[0, pl.ds(i * PITCH, SIDE), :] = spun[:, :LANES]
                weighted[1, pl.ds(i * PITCH, SIDE), :] = spun[:, LANES:]
                squares = jnp.sum(spun * spun, axis=0, keepdims=True)
                power[pl.ds(p, 1), :] = squares[:, :LANES] + squares[:, LANES:]
            return carry

        lax.fori_loop(0, BATCH // TOGETHER, several, 0)
        if b + 2 < BATCHES:
            image_load(b + 2).start()

        def turn_over(block, carry, b=b):
            for r in range(ROWS):
                if r < SIDEWAYS:
                    place = sideways(r // 4, (r % 4) * 2 + (block & 1)) + (block >> 1)
                else:
                    place = straight(block, r)
                for h in range(2):
                    lines = weighted[h, pl.ds(block * ROWS + r, BATCH, stride=PITCH), :]
                    outgoing[place, b * BATCH:(b + 1) * BATCH, h * LANES:(h + 1) * LANES] = lines.astype(BF16)
            return carry

        lax.fori_loop(0, STACK, turn_over, 0)
        if b == 0:
            pl.semaphore_wait(barrier, len(peers))
            start(tile_copies())
            start(tile_x_copies())
        start(across_copies(b))
        start(early_copies(b))

    for c in range(1, AHEAD):
        start(y_copies(c))
    for c in range(NCHUNK):
        own_copy(c).start()

    for side in range(SIDES):
        across_own(side).start()

    tiles[s] = tile[...]
    for side in range(SIDES):
        tiles_x[side, spread_at(side)] = tile[...]
    lane = lax.broadcasted_iota(jnp.int32, (8, LANES), 1)
    own_power = jnp.sum(power[...], axis=1, keepdims=True) * (1.0 / (SIDE * SIDE))
    spot = lax.broadcasted_iota(jnp.int32, (LOCAL, LANES), 1) & (LOCAL - 1)
    line = lax.broadcasted_iota(jnp.int32, (LOCAL, LANES), 0)
    own_power = jnp.sum(jnp.where(spot == line, own_power, 0.0), axis=0, keepdims=True)
    norm_tile[...] = jnp.broadcast_to(own_power, (8, LANES))
    norm_tiles[s] = jnp.broadcast_to(own_power, (8, LANES))
    start(norm_copies())

    arrive(tile_copies())
    arrive(tile_x_copies())
    natural = lax.broadcasted_iota(jnp.int32, (CLASSES, LANES), 0).astype(F32)
    which = lax.broadcasted_iota(jnp.int32, (LANES, LANES), 0)
    which_group = (which & (GROUPS - 1)).astype(F32)
    for j in range(STACK // 2):
        cols = slice(j * LANES, (j + 1) * LANES)
        both = jnp.where(lane < LOCAL, tiles[2 * j], tiles[2 * j + 1])
        hot[:, cols] = jnp.where(natural == both[0:1], 1.0, 0.0).astype(BF16)
        for side in range(SIDES):
            beside = jnp.where(lane < LOCAL, tiles_x[side, 2 * j], tiles_x[side, 2 * j + 1])
            hot_x[side, :, cols] = jnp.where(natural == beside[0:1], 1.0, 0.0).astype(BF16)
        chance = jnp.where(which < GROUPS, both[2:3], both[3:4])
        keep = (which_group == both[1:2]) & (which < 2 * GROUPS)
        mixed[:, cols] = jnp.where(keep, chance, 0.0).astype(BF16)

    def keep_lines(which, r, lines):
        at = pl.ds(pl.multiple_of((which * ROWS + r) * CLS_LOC, CLS_LOC), CLS_LOC)
        weighted[0, at, :] = lines[:, :LANES]
        weighted[1, at, :] = lines[:, LANES:]

    def result_copy(which, block):
        rows = pl.ds(block * 8, 8)
        target = (sums_out, weights_out)[which]
        return pltpu.make_async_copy(
            staged.at[which, :, rows], target.at[:, rows], result_sem.at[which, block]
        )

    def settle(which, block):
        def one_class(i, carry):
            for h in range(2):
                at = pl.ds((which * ROWS + block * 8) * CLS_LOC + i, 8, stride=CLS_LOC)
                staged[which, i, block * 8:block * 8 + 8, h * LANES:(h + 1) * LANES] = weighted[h, at, :]
            return carry

        lax.fori_loop(0, CLS_LOC, one_class, 0, unroll=8)
        result_copy(which, block).start()

    def small_start():
        arrive(norm_copies())
        total = jnp.zeros((CLASSES, LANES), F32)
        for j in range(STACK // 2):
            both = jnp.where(lane < LOCAL, tiles[2 * j], tiles[2 * j + 1])
            norm = jnp.where(lane < LOCAL, norm_tiles[2 * j], norm_tiles[2 * j + 1])
            total += jnp.where(natural == both[0:1], norm[0:1], 0.0)
        blend = lax.dot_general(hot[...], mixed[...], NT, preferred_element_type=F32)
        for owner in range(OWNERS):
            line = ((owner % 4) * 4 + owner // 4) * CLS_LOC
            small[line:line + CLS_LOC, 0:LANES] = total[owner * CLS_LOC:(owner + 1) * CLS_LOC]
            small[line:line + CLS_LOC, LANES:2 * LANES] = blend[owner * CLS_LOC:(owner + 1) * CLS_LOC]
        start(small_first_copies())

    def small_middle():
        arrive(small_first_copies())
        small_mid[...] = (
            small[pl.ds(x * 128, 128), :] + small_first[0] + small_first[1] + small_first[2]
        )
        start(small_second_copies())

    def small_end():
        arrive(small_second_copies())
        total = small_mid[pl.ds(z * CLS_LOC, CLS_LOC), :] + small_second[0] + small_second[1] + small_second[2]
        norms = jnp.sum(total[:, :LANES], axis=1, keepdims=True)
        lined = lax.broadcasted_iota(jnp.int32, (CLS_LOC, LANES), 0)
        lined = lined == lax.broadcasted_iota(jnp.int32, (CLS_LOC, LANES), 1)
        norms_out[...] = jnp.sum(jnp.where(lined, norms, 0.0), axis=0, keepdims=True)
        coef = total[:, LANES:LANES + GROUPS] + total[:, LANES + GROUPS:LANES + 2 * GROUPS]

        def weigh(r, carry):
            lines = jnp.concatenate([ctf[g, pl.ds(s * ROWS + r, 1), :] for g in range(GROUPS)], axis=0)
            spread = jnp.dot(
                coef, lines * lines, precision=lax.Precision.HIGHEST, preferred_element_type=F32
            )
            keep_lines(1, r, spread)
            return carry

        lax.fori_loop(0, ROWS, weigh, 0)
        for block in range(ROWS // 8):
            settle(1, block)

    def keep_partial(part, r, sums):
        if part == 0:
            for owner in range(OWNERS):
                line = (owner // 4) * CLS_LOC
                block = sums[owner * CLS_LOC:(owner + 1) * CLS_LOC]
                partial[owner % 4, r, line:line + CLS_LOC, :] = block
        else:
            partial[:, r] = sums.reshape(4, 128, SIDE)

    def by_class(c):
        half = CHUNKS[c] // 2
        for part in range(2):

            def add(i, carry, part=part):
                r = STARTS[c] + part * half + i
                lines = gathered[:, r].reshape(PEOPLE, SIDE)
                sums = jnp.dot(hot[...], lines, preferred_element_type=F32).astype(BF16)
                keep_partial(part, r, sums)
                return carry

            lax.fori_loop(0, half, add, 0)

    def add_first(c):
        half = CHUNKS[c] // 2
        for part, mine in enumerate((x, z)):

            def add(i, carry, part=part, mine=mine):
                r = STARTS[c] + part * half + i
                total = partial[mine, r].astype(F32)
                for d in range(3):
                    total += first_in[d, r].astype(F32)
                second[:, r] = total.reshape(4, CLS_LOC, SIDE)
                return carry

            lax.fori_loop(0, half, add, 0)

    def add_second(c):
        half = CHUNKS[c] // 2
        for part, mine in enumerate((z, x)):

            def add(i, carry, part=part, mine=mine):
                r = STARTS[c] + part * half + i
                total = second[mine, r]
                for d in range(3):
                    total += second_in[d, r - SIDEWAYS]
                keep_lines(0, r, total)
                return carry

            lax.fori_loop(0, half, add, 0)

    def side_by_class(side):
        def add(i, carry):
            r = side * 4 + i
            lines = gathered[:, r].reshape(PEOPLE, SIDE)
            sums = jnp.dot(hot_x[side], lines, preferred_element_type=F32).astype(BF16)
            keep_partial(1 - side, r, sums)
            return carry

        lax.fori_loop(0, 4, add, 0)

    def side_add_first(side):
        def add(i, carry):
            r = side * 4 + i
            total = partial[deep[side], r].astype(F32)
            for d in range(3):
                total += first_in[d, r].astype(F32)
            second[:, r] = total.reshape(4, CLS_LOC, SIDE)
            return carry

        lax.fori_loop(0, 4, add, 0)

    def side_add_second(side):
        for block in range(4):
            total = second[block, side * 4 + y]
            for d in range(3):
                total += side_second_in[side, d, block, 0]
            side_third[side, block] = total

    def side_keep(side):
        keep_lines(0, side * 4 + wide[side], side_third[side, wide[side]])
        for d in (1, 2, 3):
            keep_lines(0, side * 4 + (wide[side] + 4 - d) % 4, side_third_in[side, d - 1])

    for c in range(NCHUNK + SECOND_LAG):
        if c < NCHUNK:
            if c == 0:
                for b in range(BATCHES):
                    arrive(early_copies(b))
            else:
                arrive(y_copies(c))
            if c + AHEAD < NCHUNK:
                start(y_copies(c + AHEAD))
            own_copy(c).wait()
            by_class(c)
            start(first_copies(c))
        if c == 0:
            for b in range(BATCHES):
                arrive(across_copies(b))
            for side in range(SIDES):
                across_own(side).wait()
                side_by_class(side)
                start(side_first(side))
        if c == SIDE_LAGS[0]:
            for side in range(SIDES):
                arrive(side_first(side))
                side_add_first(side)
                start(side_second(side))
        if c == SIDE_LAGS[1]:
            for side in range(SIDES):
                arrive(side_second(side))
                side_add_second(side)
                start(side_last(side))
        if c == NCHUNK:
            for side in range(SIDES):
                arrive(side_last(side))
                side_keep(side)
            settle(0, 0)
        if c == 0:
            small_start()
        if c == 1:
            small_middle()
        if 0 <= c - FIRST_LAG < NCHUNK:
            arrive(first_copies(c - FIRST_LAG))
            add_first(c - FIRST_LAG)
            start(second_copies(c - FIRST_LAG))
        if c == 2:
            small_end()
        if 0 <= c - SECOND_LAG < NCHUNK:
            arrive(second_copies(c - SECOND_LAG))
            add_second(c - SECOND_LAG)
            begun = STARTS[c - SECOND_LAG]
            for block in range(begun // 8, (begun + CHUNKS[c - SECOND_LAG]) // 8):
                settle(0, block)

    leave(tile_copies())
    leave(norm_copies())
    for b in range(BATCHES):
        leave(early_copies(b))
    for c in range(NCHUNK):
        if c > 0:
            leave(y_copies(c))
        leave(first_copies(c))
        leave(second_copies(c))
    leave(small_first_copies())
    leave(small_second_copies())
    leave(tile_x_copies())
    for b in range(BATCHES):
        leave(across_copies(b))
    for side in range(SIDES):
        leave(side_first(side))
        leave(side_second(side))
        leave(side_last(side))
    for which in range(2):
        for block in range(ROWS // 8):
            result_copy(which, block).wait()


def hand_over(sums, weights, norms, sums_out, weights_out, norms_out, held, in_sem, out_sem):
    size = CLS_LOC // PIECES
    arriving, leaving = [], []
    for n in range(PIECES):
        part = pl.ds(n * size, size)
        for which, (src, dst) in enumerate(((sums, sums_out), (weights, weights_out))):
            arriving.append(pltpu.make_async_copy(src.at[part], held.at[which, part], in_sem.at[which, n]))
            leaving.append(pltpu.make_async_copy(held.at[which, part], dst.at[part], out_sem.at[which, n]))
    for copy in arriving:
        copy.start()
    norms_out[...] = norms[0, :CLS_LOC]
    for here, there in zip(arriving, leaving):
        here.wait()
        there.start()
    for copy in leaving:
        copy.wait()


def per_device(particles, classes, angles, groups, posterior, left_maps, right_maps, ctf_table):
    smem = pl.BlockSpec(memory_space=pltpu.SMEM)
    vmem = pl.BlockSpec(memory_space=pltpu.VMEM)
    hbm = pl.BlockSpec(memory_space=pl.ANY)
    n = len(STACK_STEPS)
    dma = pltpu.SemaphoreType.DMA
    sums, weights, norms = pl.pallas_call(
        body,
        out_shape=(
            jax.ShapeDtypeStruct((CLS_LOC, ROWS, SIDE), F32),
            jax.ShapeDtypeStruct((CLS_LOC, ROWS, SIDE), F32),
            jax.ShapeDtypeStruct((1, LANES), F32),
        ),
        in_specs=[smem, smem, vmem, vmem, vmem, hbm, hbm, hbm, hbm],
        out_specs=(hbm, hbm, vmem),
        scratch_shapes=[
            pltpu.VMEM((ANGLES, SIDE, SIDE), BF16),
            pltpu.VMEM((ANGLES, SIDE, SIDE), BF16),
            pltpu.VMEM((GROUPS, SIDE, SIDE), F32),
            pltpu.VMEM((2, BATCH, SIDE, SIDE), BF16),
            pltpu.VMEM((2, BATCH * PITCH, LANES), F32),
            pltpu.VMEM((LOCAL, LANES), F32),
            pltpu.VMEM((SIDE, LOCAL, SIDE), BF16),
            pltpu.VMEM((STACK, ROWS, LOCAL, SIDE), BF16),
            pltpu.VMEM((CLASSES, PEOPLE), BF16),
            pltpu.VMEM((SIDES, CLASSES, PEOPLE), BF16),
            pltpu.VMEM((LANES, PEOPLE), BF16),
            pltpu.VMEM((8, LANES), F32),
            pltpu.SMEM((8, LANES), F32),
            pltpu.VMEM((STACK, 8, LANES), F32),
            pltpu.VMEM((SIDES, STACK, 8, LANES), F32),
            pltpu.VMEM((8, LANES), F32),
            pltpu.VMEM((STACK, 8, LANES), F32),
            pltpu.VMEM((4, ROWS, 128, SIDE), BF16),
            pltpu.VMEM((3, ROWS, 128, SIDE), BF16),
            pltpu.VMEM((4, ROWS, CLS_LOC, SIDE), F32),
            pltpu.VMEM((3, STRAIGHT, CLS_LOC, SIDE), F32),
            pltpu.VMEM((CLASSES, 2 * LANES), F32),
            pltpu.VMEM((3, 128, 2 * LANES), F32),
            pltpu.VMEM((128, 2 * LANES), F32),
            pltpu.VMEM((3, CLS_LOC, 2 * LANES), F32),
            pltpu.VMEM((2, CLS_LOC, ROWS, SIDE), F32),
            pltpu.VMEM((SIDES, 3, 4, 1, CLS_LOC, SIDE), F32),
            pltpu.VMEM((SIDES, 4, CLS_LOC, SIDE), F32),
            pltpu.VMEM((SIDES, 3, CLS_LOC, SIDE), F32),
            dma((4,)), dma((2,)), dma((NCHUNK,)),
            dma((n,)), dma((n,)), dma((n,)), dma((n,)),
            dma((BATCHES, n)), dma((BATCHES, n)), dma((NCHUNK, n)), dma((NCHUNK, n)),
            dma((NCHUNK, 2, 3)), dma((NCHUNK, 2, 3)), dma((NCHUNK, 2, 3)), dma((NCHUNK, 2, 3)),
            dma((2, 3)), dma((2, 3)), dma((2, ROWS // 8)),
            dma((BATCHES, SIDES, n)), dma((BATCHES, SIDES, n)), dma((SIDES, n)), dma((SIDES, n)),
            dma((SIDES, 3, 3)), dma((SIDES, 3, 3)), dma((SIDES,)),
        ],
        compiler_params=pltpu.CompilerParams(
            collective_id=0, has_side_effects=True, vmem_limit_bytes=63 * 1024 * 1024
        ),
        name="class_sums",
    )(angles, groups, classes.reshape(1, LOCAL), groups.reshape(1, LOCAL), posterior.T, particles, left_maps, right_maps, ctf_table)
    shape = jax.ShapeDtypeStruct((CLS_LOC, ROWS, SIDE), F32)
    return pl.pallas_call(
        hand_over,
        out_shape=(shape, shape, jax.ShapeDtypeStruct((CLS_LOC,), F32)),
        in_specs=[hbm, hbm, vmem],
        out_specs=(hbm, hbm, vmem),
        scratch_shapes=[pltpu.VMEM((2, CLS_LOC, ROWS, SIDE), F32), dma((2, PIECES)), dma((2, PIECES))],
        compiler_params=pltpu.CompilerParams(vmem_limit_bytes=8 * 1024 * 1024),
        name="hand_over",
    )(sums, weights, norms)


def solution(mesh):
    return jax.shard_map(
        per_device,
        mesh=mesh,
        in_specs=(
            P(("stack", "cls"), None, None),
            P(("stack", "cls")),
            P(("stack", "cls")),
            P(("stack", "cls")),
            P(("stack", "cls"), None),
            P(),
            P(),
            P(),
        ),
        out_specs=(P("cls", "stack", None), P("cls", "stack", None), P("cls")),
        check_vma=False,
    )
```

```python
import jax
import jax.numpy as jnp
from jax import lax
from jax.experimental import pallas as pl
from jax.experimental.pallas import tpu as pltpu
from jax.sharding import PartitionSpec as P

MESH = pl.DeviceIdType.MESH
F32 = jnp.float32
BF16 = jnp.bfloat16
SIDE = 256
ANGLES = 16
GROUPS = 16
LOCAL = 64
BATCH = 16
BATCHES = LOCAL // BATCH
STACK = 8
OWNERS = 16
CLS_LOC = 32
CLASSES = OWNERS * CLS_LOC
ROWS = SIDE // STACK
PEOPLE = STACK * LOCAL
PITCH = SIDE + 8
TOGETHER = 8
PIECES = 4
LANES = 128
CHUNKS = (4, 4, 4, 4, 4, 2, 2)
SIDEWAYS = 8
SIDES = 2
STRAIGHT = ROWS - SIDEWAYS
STARTS = tuple(SIDEWAYS + sum(CHUNKS[:n]) for n in range(len(CHUNKS)))
NCHUNK = len(CHUNKS)
AHEAD = 2
FIRST_LAG = 1
SECOND_LAG = 2
SIDE_LAGS = (2, 4)
STACK_STEPS = tuple((dy, dc) for dy in (2, 1, 3, 0) for dc in (0, 1) if (dy, dc) != (0, 0))
ACROSS_STEPS = tuple((dx, dc) for dx in (2, 1, 3, 0) for dc in (0, 1) if (dx, dc) != (0, 0))
NT = (((1,), (1,)), ((), ()))


def body(
    angles, groups, class_row, group_row, chance_rows, particles, left_hbm, right_hbm, ctf_hbm,
    sums_out, weights_out, norms_out,
    left, right, ctf, images, weighted, power, outgoing, gathered,
    hot, hot_x, mixed, tile, posterior, tiles, tiles_x, norm_tile, norm_tiles,
    partial, first_in, second, second_in,
    small, small_first, small_mid, small_second, staged, side_second_in, side_third, side_third_in,
    load_sem, image_sem, own_sem,
    tile_send, tile_recv, norm_send, norm_recv,
    early_send, early_recv, y_send, y_recv,
    first_send, first_recv, second_send, second_recv,
    small_send, small_recv, result_sem,
    across_send, across_recv, tile_x_send, tile_x_recv, side_send, side_recv, side_own_sem,
):
    s = lax.axis_index("stack")
    k = lax.axis_index("cls")
    y, core = s // 2, s % 2
    z, x = k // 4, k % 4

    def along_stack(step):
        return (((y + step[0]) % 4) * 2 + (core + step[1]) % 2, k)

    def across(side, step):
        there = (z * 4 + (x + step[0]) % 4, ((z + step[0]) % 4) * 4 + x)[side]
        return (y * 2 + (core + step[1]) % 2, there)

    def along_x(d):
        return (s, z * 4 + (x + d) % 4)

    def along_z(d):
        return (s, ((z + d) % 4) * 4 + x)

    def along_y(d):
        return (((y + d) % 4) * 2 + core, k)

    wide, deep = (x, z), (z, x)
    along_wide, along_deep = (along_x, along_z), (along_z, along_x)

    def spread_at(side):
        return wide[side] * 2 + core


    loads = [
        pltpu.make_async_copy(left_hbm, left, load_sem.at[0]),
        pltpu.make_async_copy(right_hbm, right, load_sem.at[1]),
        pltpu.make_async_copy(ctf_hbm, ctf, load_sem.at[2]),
    ]

    def image_load(b):
        return pltpu.make_async_copy(
            particles.at[pl.ds(b * BATCH, BATCH)], images.at[b % 2], image_sem.at[b % 2]
        )

    loads[1].start()
    image_load(0).start()
    loads[0].start()
    loads[2].start()
    image_load(1).start()

    labels = jnp.concatenate(
        [class_row[...].astype(F32), group_row[...].astype(F32), chance_rows[...].astype(F32)], axis=0
    )
    tile[0:4, :] = jnp.concatenate([labels, labels], axis=1)
    tile[4:8, :] = jnp.zeros((4, LANES), F32)
    to_scalars = pltpu.make_async_copy(tile, posterior, load_sem.at[3])
    to_scalars.start()

    barrier = pltpu.get_barrier_semaphore()
    peers = [along_stack(step) for step in STACK_STEPS]
    for side in range(SIDES):
        peers += [across(side, step) for step in ACROSS_STEPS if step[0] != 0 and step[1] != 0]
    peers += [along_x(d) for d in (1, 2, 3)] + [along_z(d) for d in (1, 2, 3)]
    for peer in peers:
        pl.semaphore_signal(barrier, inc=1, device_id=peer, device_id_type=MESH)

    def remote(src, dst, send, recv, peer):
        return pltpu.make_async_remote_copy(
            src_ref=src, dst_ref=dst, send_sem=send, recv_sem=recv, device_id=peer, device_id_type=MESH
        )

    def tile_copies():
        return [
            remote(tile, tiles.at[s], tile_send.at[n], tile_recv.at[n], along_stack(step))
            for n, step in enumerate(STACK_STEPS)
        ]

    def tile_x_copies():
        return [
            remote(
                tile, tiles_x.at[side, spread_at(side)],
                tile_x_send.at[side, n], tile_x_recv.at[side, n], across(side, step),
            )
            for side in range(SIDES)
            for n, step in enumerate(ACROSS_STEPS)
        ]

    def sideways(side, spot):
        return side * STACK * 4 + spot * 4

    def across_copies(b):
        out = []
        for n, step in enumerate(ACROSS_STEPS):
            for side in range(SIDES):
                spot = ((wide[side] + step[0]) % 4) * 2 + (core + step[1]) % 2
                out.append(
                    remote(
                        outgoing.at[pl.ds(sideways(side, spot), 4), pl.ds(b * BATCH, BATCH)],
                        gathered.at[spread_at(side), pl.ds(side * 4, 4), pl.ds(b * BATCH, BATCH)],
                        across_send.at[b, side, n], across_recv.at[b, side, n], across(side, step),
                    )
                )
        return out

    def across_own(side):
        return pltpu.make_async_copy(
            outgoing.at[pl.ds(sideways(side, spread_at(side)), 4)],
            gathered.at[spread_at(side), pl.ds(side * 4, 4)],
            side_own_sem.at[side],
        )

    def side_first(side):
        rows = pl.ds(side * 4, 4)
        return [
            remote(
                partial.at[(deep[side] + d) % 4, rows], first_in.at[d - 1, rows],
                side_send.at[side, 0, d - 1], side_recv.at[side, 0, d - 1], along_deep[side](d),
            )
            for d in (1, 2, 3)
        ]

    def side_second(side):
        return [
            remote(
                second.at[:, pl.ds(side * 4 + (y + d) % 4, 1)], side_second_in.at[side, d - 1],
                side_send.at[side, 1, d - 1], side_recv.at[side, 1, d - 1], along_y(d),
            )
            for d in (1, 2, 3)
        ]

    def side_last(side):
        return [
            remote(
                side_third.at[side, (wide[side] + d) % 4], side_third_in.at[side, d - 1],
                side_send.at[side, 2, d - 1], side_recv.at[side, 2, d - 1], along_wide[side](d),
            )
            for d in (1, 2, 3)
        ]

    def norm_copies():
        return [
            remote(norm_tile, norm_tiles.at[s], norm_send.at[n], norm_recv.at[n], along_stack(step))
            for n, step in enumerate(STACK_STEPS)
        ]

    def straight(block, row):
        return STACK * SIDEWAYS + block * STRAIGHT + row - SIDEWAYS

    def early_copies(b):
        rows = CHUNKS[0]
        out = []
        for n, step in enumerate(STACK_STEPS):
            peer = along_stack(step)
            out.append(
                remote(
                    outgoing.at[pl.ds(straight(peer[0], STARTS[0]), rows), pl.ds(b * BATCH, BATCH)],
                    gathered.at[s, pl.ds(STARTS[0], rows), pl.ds(b * BATCH, BATCH)],
                    early_send.at[b, n], early_recv.at[b, n], peer,
                )
            )
        return out

    def y_copies(c):
        start, rows = STARTS[c], CHUNKS[c]
        out = []
        for n, step in enumerate(STACK_STEPS):
            peer = along_stack(step)
            out.append(
                remote(
                    outgoing.at[pl.ds(straight(peer[0], start), rows)],
                    gathered.at[s, pl.ds(start, rows)],
                    y_send.at[c, n], y_recv.at[c, n], peer,
                )
            )
        return out

    def own_copy(c):
        start, rows = STARTS[c], CHUNKS[c]
        return pltpu.make_async_copy(
            outgoing.at[pl.ds(straight(s, start), rows)],
            gathered.at[s, pl.ds(start, rows)],
            own_sem.at[c],
        )

    def first_copies(c):
        half = CHUNKS[c] // 2
        out = []
        for d in (1, 2, 3):
            for part, (hop, spot) in enumerate(((along_x, (x + d) % 4), (along_z, (z + d) % 4))):
                rows = pl.ds(STARTS[c] + part * half, half)
                out.append(
                    remote(
                        partial.at[spot, rows], first_in.at[d - 1, rows],
                        first_send.at[c, part, d - 1], first_recv.at[c, part, d - 1], hop(d),
                    )
                )
        return out

    def second_copies(c):
        half = CHUNKS[c] // 2
        out = []
        for d in (1, 2, 3):
            for part, (hop, spot) in enumerate(((along_z, (z + d) % 4), (along_x, (x + d) % 4))):
                rows = pl.ds(STARTS[c] + part * half, half)
                out.append(
                    remote(
                        second.at[spot, rows], second_in.at[d - 1, pl.ds(STARTS[c] - SIDEWAYS + part * half, half)],
                        second_send.at[c, part, d - 1], second_recv.at[c, part, d - 1], hop(d),
                    )
                )
        return out

    def small_first_copies():
        return [
            remote(
                small.at[pl.ds(((x + d) % 4) * 128, 128)], small_first.at[d - 1],
                small_send.at[0, d - 1], small_recv.at[0, d - 1], along_x(d),
            )
            for d in (1, 2, 3)
        ]

    def small_second_copies():
        return [
            remote(
                small_mid.at[pl.ds(((z + d) % 4) * CLS_LOC, CLS_LOC)], small_second.at[d - 1],
                small_send.at[1, d - 1], small_recv.at[1, d - 1], along_z(d),
            )
            for d in (1, 2, 3)
        ]

    def start(copies):
        for copy in copies:
            copy.start()

    def arrive(copies):
        for copy in copies:
            copy.wait_recv()

    def leave(copies):
        for copy in copies:
            copy.wait_send()

    for b in range(BATCHES):
        if b == 0:
            loads[1].wait()
        image_load(b).wait()
        if b == 0:
            loads[0].wait()
            loads[2].wait()
            to_scalars.wait()

        def several(n, carry, b=b):
            spots = [n * TOGETHER + m for m in range(TOGETHER)]
            turns, sheared = [], []
            for i in spots:
                turn = angles[b * BATCH + i]
                turns.append((turn, (turn + 1) & (ANGLES - 1)))
            for i, near in zip(spots, turns):
                image = images[b % 2, i]
                sheared.append([
                    lax.dot_general(image, right[turn], NT, preferred_element_type=F32).astype(BF16)
                    for turn in near
                ])
            for i, near, pair in zip(spots, turns, sheared):
                p = b * BATCH + i
                spun = posterior[2, p] * jnp.dot(left[near[0]], pair[0], preferred_element_type=F32)
                spun += posterior[3, p] * jnp.dot(left[near[1]], pair[1], preferred_element_type=F32)
                spun = ctf[groups[p]] * spun
                weighted[0, pl.ds(i * PITCH, SIDE), :] = spun[:, :LANES]
                weighted[1, pl.ds(i * PITCH, SIDE), :] = spun[:, LANES:]
                squares = jnp.sum(spun * spun, axis=0, keepdims=True)
                power[pl.ds(p, 1), :] = squares[:, :LANES] + squares[:, LANES:]
            return carry

        lax.fori_loop(0, BATCH // TOGETHER, several, 0)
        if b + 2 < BATCHES:
            image_load(b + 2).start()

        def turn_over(block, carry, b=b):
            for r in range(ROWS):
                if r < SIDEWAYS:
                    place = sideways(r // 4, (r % 4) * 2 + (block & 1)) + (block >> 1)
                else:
                    place = straight(block, r)
                for h in range(2):
                    lines = weighted[h, pl.ds(block * ROWS + r, BATCH, stride=PITCH), :]
                    outgoing[place, b * BATCH:(b + 1) * BATCH, h * LANES:(h + 1) * LANES] = lines.astype(BF16)
            return carry

        lax.fori_loop(0, STACK, turn_over, 0)
        if b == 0:
            pl.semaphore_wait(barrier, len(peers))
            start(tile_copies())
            start(tile_x_copies())
        start(across_copies(b))
        start(early_copies(b))

    for c in range(1, AHEAD):
        start(y_copies(c))
    for c in range(NCHUNK):
        own_copy(c).start()

    for side in range(SIDES):
        across_own(side).start()

    tiles[s] = tile[...]
    for side in range(SIDES):
        tiles_x[side, spread_at(side)] = tile[...]
    lane = lax.broadcasted_iota(jnp.int32, (8, LANES), 1)
    own_power = jnp.sum(power[...], axis=1, keepdims=True) * (1.0 / (SIDE * SIDE))
    spot = lax.broadcasted_iota(jnp.int32, (LOCAL, LANES), 1) & (LOCAL - 1)
    line = lax.broadcasted_iota(jnp.int32, (LOCAL, LANES), 0)
    own_power = jnp.sum(jnp.where(spot == line, own_power, 0.0), axis=0, keepdims=True)
    norm_tile[...] = jnp.broadcast_to(own_power, (8, LANES))
    norm_tiles[s] = jnp.broadcast_to(own_power, (8, LANES))
    start(norm_copies())

    arrive(tile_copies())
    arrive(tile_x_copies())
    natural = lax.broadcasted_iota(jnp.int32, (CLASSES, LANES), 0).astype(F32)
    which = lax.broadcasted_iota(jnp.int32, (LANES, LANES), 0)
    which_group = (which & (GROUPS - 1)).astype(F32)
    for j in range(STACK // 2):
        cols = slice(j * LANES, (j + 1) * LANES)
        both = jnp.where(lane < LOCAL, tiles[2 * j], tiles[2 * j + 1])
        hot[:, cols] = jnp.where(natural == both[0:1], 1.0, 0.0).astype(BF16)
        for side in range(SIDES):
            beside = jnp.where(lane < LOCAL, tiles_x[side, 2 * j], tiles_x[side, 2 * j + 1])
            hot_x[side, :, cols] = jnp.where(natural == beside[0:1], 1.0, 0.0).astype(BF16)
        chance = jnp.where(which < GROUPS, both[2:3], both[3:4])
        keep = (which_group == both[1:2]) & (which < 2 * GROUPS)
        mixed[:, cols] = jnp.where(keep, chance, 0.0).astype(BF16)

    def keep_lines(which, r, lines):
        at = pl.ds(pl.multiple_of((which * ROWS + r) * CLS_LOC, CLS_LOC), CLS_LOC)
        weighted[0, at, :] = lines[:, :LANES]
        weighted[1, at, :] = lines[:, LANES:]

    def result_copy(which, block):
        rows = pl.ds(block * 8, 8)
        target = (sums_out, weights_out)[which]
        return pltpu.make_async_copy(
            staged.at[which, :, rows], target.at[:, rows], result_sem.at[which, block]
        )

    def settle(which, block):
        def one_class(i, carry):
            for h in range(2):
                at = pl.ds((which * ROWS + block * 8) * CLS_LOC + i, 8, stride=CLS_LOC)
                staged[which, i, block * 8:block * 8 + 8, h * LANES:(h + 1) * LANES] = weighted[h, at, :]
            return carry

        lax.fori_loop(0, CLS_LOC, one_class, 0, unroll=8)
        result_copy(which, block).start()

    def small_start():
        arrive(norm_copies())
        total = jnp.zeros((CLASSES, LANES), F32)
        for j in range(STACK // 2):
            both = jnp.where(lane < LOCAL, tiles[2 * j], tiles[2 * j + 1])
            norm = jnp.where(lane < LOCAL, norm_tiles[2 * j], norm_tiles[2 * j + 1])
            total += jnp.where(natural == both[0:1], norm[0:1], 0.0)
        blend = lax.dot_general(hot[...], mixed[...], NT, preferred_element_type=F32)
        for owner in range(OWNERS):
            line = ((owner % 4) * 4 + owner // 4) * CLS_LOC
            small[line:line + CLS_LOC, 0:LANES] = total[owner * CLS_LOC:(owner + 1) * CLS_LOC]
            small[line:line + CLS_LOC, LANES:2 * LANES] = blend[owner * CLS_LOC:(owner + 1) * CLS_LOC]
        start(small_first_copies())

    def small_middle():
        arrive(small_first_copies())
        small_mid[...] = (
            small[pl.ds(x * 128, 128), :] + small_first[0] + small_first[1] + small_first[2]
        )
        start(small_second_copies())

    def small_end():
        arrive(small_second_copies())
        total = small_mid[pl.ds(z * CLS_LOC, CLS_LOC), :] + small_second[0] + small_second[1] + small_second[2]
        norms = jnp.sum(total[:, :LANES], axis=1, keepdims=True)
        lined = lax.broadcasted_iota(jnp.int32, (CLS_LOC, LANES), 0)
        lined = lined == lax.broadcasted_iota(jnp.int32, (CLS_LOC, LANES), 1)
        norms_out[...] = jnp.sum(jnp.where(lined, norms, 0.0), axis=0, keepdims=True)
        coef = total[:, LANES:LANES + GROUPS] + total[:, LANES + GROUPS:LANES + 2 * GROUPS]

        def weigh(r, carry):
            lines = jnp.concatenate([ctf[g, pl.ds(s * ROWS + r, 1), :] for g in range(GROUPS)], axis=0)
            spread = jnp.dot(
                coef, lines * lines, precision=lax.Precision.HIGHEST, preferred_element_type=F32
            )
            keep_lines(1, r, spread)
            return carry

        lax.fori_loop(0, ROWS, weigh, 0)
        for block in range(ROWS // 8):
            settle(1, block)

    def keep_partial(part, r, sums):
        if part == 0:
            for owner in range(OWNERS):
                line = (owner // 4) * CLS_LOC
                block = sums[owner * CLS_LOC:(owner + 1) * CLS_LOC]
                partial[owner % 4, r, line:line + CLS_LOC, :] = block
        else:
            partial[:, r] = sums.reshape(4, 128, SIDE)

    def by_class(c):
        half = CHUNKS[c] // 2
        for part in range(2):

            def add(i, carry, part=part):
                r = STARTS[c] + part * half + i
                lines = gathered[:, r].reshape(PEOPLE, SIDE)
                sums = jnp.dot(hot[...], lines, preferred_element_type=F32).astype(BF16)
                keep_partial(part, r, sums)
                return carry

            lax.fori_loop(0, half, add, 0)

    def add_first(c):
        half = CHUNKS[c] // 2
        for part, mine in enumerate((x, z)):

            def add(i, carry, part=part, mine=mine):
                r = STARTS[c] + part * half + i
                total = partial[mine, r].astype(F32)
                for d in range(3):
                    total += first_in[d, r].astype(F32)
                second[:, r] = total.reshape(4, CLS_LOC, SIDE)
                return carry

            lax.fori_loop(0, half, add, 0)

    def add_second(c):
        half = CHUNKS[c] // 2
        for part, mine in enumerate((z, x)):

            def add(i, carry, part=part, mine=mine):
                r = STARTS[c] + part * half + i
                total = second[mine, r]
                for d in range(3):
                    total += second_in[d, r - SIDEWAYS]
                keep_lines(0, r, total)
                return carry

            lax.fori_loop(0, half, add, 0)

    def side_by_class(side):
        def add(i, carry):
            r = side * 4 + i
            lines = gathered[:, r].reshape(PEOPLE, SIDE)
            sums = jnp.dot(hot_x[side], lines, preferred_element_type=F32).astype(BF16)
            keep_partial(1 - side, r, sums)
            return carry

        lax.fori_loop(0, 4, add, 0)

    def side_add_first(side):
        def add(i, carry):
            r = side * 4 + i
            total = partial[deep[side], r].astype(F32)
            for d in range(3):
                total += first_in[d, r].astype(F32)
            second[:, r] = total.reshape(4, CLS_LOC, SIDE)
            return carry

        lax.fori_loop(0, 4, add, 0)

    def side_add_second(side):
        for block in range(4):
            total = second[block, side * 4 + y]
            for d in range(3):
                total += side_second_in[side, d, block, 0]
            side_third[side, block] = total

    def side_keep(side):
        keep_lines(0, side * 4 + wide[side], side_third[side, wide[side]])
        for d in (1, 2, 3):
            keep_lines(0, side * 4 + (wide[side] + 4 - d) % 4, side_third_in[side, d - 1])

    for c in range(NCHUNK + SECOND_LAG):
        if c < NCHUNK:
            if c == 0:
                for b in range(BATCHES):
                    arrive(early_copies(b))
            else:
                arrive(y_copies(c))
            if c + AHEAD < NCHUNK:
                start(y_copies(c + AHEAD))
            own_copy(c).wait()
            by_class(c)
            start(first_copies(c))
        if c == 0:
            for b in range(BATCHES):
                arrive(across_copies(b))
            for side in range(SIDES):
                across_own(side).wait()
                side_by_class(side)
                start(side_first(side))
        if c == SIDE_LAGS[0]:
            for side in range(SIDES):
                arrive(side_first(side))
                side_add_first(side)
                start(side_second(side))
        if c == SIDE_LAGS[1]:
            for side in range(SIDES):
                arrive(side_second(side))
                side_add_second(side)
                start(side_last(side))
        if c == NCHUNK:
            for side in range(SIDES):
                arrive(side_last(side))
                side_keep(side)
            settle(0, 0)
        if c == 0:
            small_start()
        if c == 1:
            small_middle()
        if 0 <= c - FIRST_LAG < NCHUNK:
            arrive(first_copies(c - FIRST_LAG))
            add_first(c - FIRST_LAG)
            start(second_copies(c - FIRST_LAG))
        if c == 2:
            small_end()
        if 0 <= c - SECOND_LAG < NCHUNK:
            arrive(second_copies(c - SECOND_LAG))
            add_second(c - SECOND_LAG)
            begun = STARTS[c - SECOND_LAG]
            for block in range(begun // 8, (begun + CHUNKS[c - SECOND_LAG]) // 8):
                settle(0, block)

    leave(tile_copies())
    leave(norm_copies())
    for b in range(BATCHES):
        leave(early_copies(b))
    for c in range(NCHUNK):
        if c > 0:
            leave(y_copies(c))
        leave(first_copies(c))
        leave(second_copies(c))
    leave(small_first_copies())
    leave(small_second_copies())
    leave(tile_x_copies())
    for b in range(BATCHES):
        leave(across_copies(b))
    for side in range(SIDES):
        leave(side_first(side))
        leave(side_second(side))
        leave(side_last(side))
    for which in range(2):
        for block in range(ROWS // 8):
            result_copy(which, block).wait()


def hand_over(sums, weights, norms, sums_out, weights_out, norms_out, held, in_sem, out_sem):
    size = CLS_LOC // PIECES
    arriving, leaving = [], []
    for n in range(PIECES):
        part = pl.ds(n * size, size)
        for which, (src, dst) in enumerate(((sums, sums_out), (weights, weights_out))):
            arriving.append(pltpu.make_async_copy(src.at[part], held.at[which, part], in_sem.at[which, n]))
            leaving.append(pltpu.make_async_copy(held.at[which, part], dst.at[part], out_sem.at[which, n]))
    for copy in arriving:
        copy.start()
    norms_out[...] = norms[0, :CLS_LOC]
    for here, there in zip(arriving, leaving):
        here.wait()
        there.start()
    for copy in leaving:
        copy.wait()


def per_device(particles, classes, angles, groups, posterior, left_maps, right_maps, ctf_table):
    smem = pl.BlockSpec(memory_space=pltpu.SMEM)
    vmem = pl.BlockSpec(memory_space=pltpu.VMEM)
    hbm = pl.BlockSpec(memory_space=pl.ANY)
    n = len(STACK_STEPS)
    dma = pltpu.SemaphoreType.DMA
    sums, weights, norms = pl.pallas_call(
        body,
        out_shape=(
            jax.ShapeDtypeStruct((CLS_LOC, ROWS, SIDE), F32),
            jax.ShapeDtypeStruct((CLS_LOC, ROWS, SIDE), F32),
            jax.ShapeDtypeStruct((1, LANES), F32),
        ),
        in_specs=[smem, smem, vmem, vmem, vmem, hbm, hbm, hbm, hbm],
        out_specs=(hbm, hbm, vmem),
        scratch_shapes=[
            pltpu.VMEM((ANGLES, SIDE, SIDE), BF16),
            pltpu.VMEM((ANGLES, SIDE, SIDE), BF16),
            pltpu.VMEM((GROUPS, SIDE, SIDE), F32),
            pltpu.VMEM((2, BATCH, SIDE, SIDE), BF16),
            pltpu.VMEM((2, BATCH * PITCH, LANES), F32),
            pltpu.VMEM((LOCAL, LANES), F32),
            pltpu.VMEM((SIDE, LOCAL, SIDE), BF16),
            pltpu.VMEM((STACK, ROWS, LOCAL, SIDE), BF16),
            pltpu.VMEM((CLASSES, PEOPLE), BF16),
            pltpu.VMEM((SIDES, CLASSES, PEOPLE), BF16),
            pltpu.VMEM((LANES, PEOPLE), BF16),
            pltpu.VMEM((8, LANES), F32),
            pltpu.SMEM((8, LANES), F32),
            pltpu.VMEM((STACK, 8, LANES), F32),
            pltpu.VMEM((SIDES, STACK, 8, LANES), F32),
            pltpu.VMEM((8, LANES), F32),
            pltpu.VMEM((STACK, 8, LANES), F32),
            pltpu.VMEM((4, ROWS, 128, SIDE), BF16),
            pltpu.VMEM((3, ROWS, 128, SIDE), BF16),
            pltpu.VMEM((4, ROWS, CLS_LOC, SIDE), F32),
            pltpu.VMEM((3, STRAIGHT, CLS_LOC, SIDE), F32),
            pltpu.VMEM((CLASSES, 2 * LANES), F32),
            pltpu.VMEM((3, 128, 2 * LANES), F32),
            pltpu.VMEM((128, 2 * LANES), F32),
            pltpu.VMEM((3, CLS_LOC, 2 * LANES), F32),
            pltpu.VMEM((2, CLS_LOC, ROWS, SIDE), F32),
            pltpu.VMEM((SIDES, 3, 4, 1, CLS_LOC, SIDE), F32),
            pltpu.VMEM((SIDES, 4, CLS_LOC, SIDE), F32),
            pltpu.VMEM((SIDES, 3, CLS_LOC, SIDE), F32),
            dma((4,)), dma((2,)), dma((NCHUNK,)),
            dma((n,)), dma((n,)), dma((n,)), dma((n,)),
            dma((BATCHES, n)), dma((BATCHES, n)), dma((NCHUNK, n)), dma((NCHUNK, n)),
            dma((NCHUNK, 2, 3)), dma((NCHUNK, 2, 3)), dma((NCHUNK, 2, 3)), dma((NCHUNK, 2, 3)),
            dma((2, 3)), dma((2, 3)), dma((2, ROWS // 8)),
            dma((BATCHES, SIDES, n)), dma((BATCHES, SIDES, n)), dma((SIDES, n)), dma((SIDES, n)),
            dma((SIDES, 3, 3)), dma((SIDES, 3, 3)), dma((SIDES,)),
        ],
        compiler_params=pltpu.CompilerParams(
            collective_id=0, has_side_effects=True, vmem_limit_bytes=63 * 1024 * 1024
        ),
        name="class_sums",
    )(angles, groups, classes.reshape(1, LOCAL), groups.reshape(1, LOCAL), posterior.T, particles, left_maps, right_maps, ctf_table)
    shape = jax.ShapeDtypeStruct((CLS_LOC, ROWS, SIDE), F32)
    return pl.pallas_call(
        hand_over,
        out_shape=(shape, shape, jax.ShapeDtypeStruct((CLS_LOC,), F32)),
        in_specs=[hbm, hbm, vmem],
        out_specs=(hbm, hbm, vmem),
        scratch_shapes=[pltpu.VMEM((2, CLS_LOC, ROWS, SIDE), F32), dma((2, PIECES)), dma((2, PIECES))],
        compiler_params=pltpu.CompilerParams(vmem_limit_bytes=63 * 1024 * 1024),
        name="hand_over",
    )(sums, weights, norms)


def solution(mesh):
    return jax.shard_map(
        per_device,
        mesh=mesh,
        in_specs=(
            P(("stack", "cls"), None, None),
            P(("stack", "cls")),
            P(("stack", "cls")),
            P(("stack", "cls")),
            P(("stack", "cls"), None),
            P(),
            P(),
            P(),
        ),
        out_specs=(P("cls", "stack", None), P("cls", "stack", None), P("cls")),
        check_vma=False,
    )
```

```python
import jax
import jax.numpy as jnp
from jax import lax
from jax.experimental import pallas as pl
from jax.experimental.pallas import tpu as pltpu
from jax.sharding import PartitionSpec as P

MESH = pl.DeviceIdType.MESH
F32 = jnp.float32
BF16 = jnp.bfloat16
SIDE = 256
ANGLES = 16
GROUPS = 16
LOCAL = 64
BATCH = 16
BATCHES = LOCAL // BATCH
STACK = 8
OWNERS = 16
CLS_LOC = 32
CLASSES = OWNERS * CLS_LOC
ROWS = SIDE // STACK
PEOPLE = STACK * LOCAL
PITCH = SIDE + 8
TOGETHER = 8
PIECES = 4
LANES = 128
CHUNKS = (4, 4, 4, 4, 4, 4)
SIDEWAYS = 8
SIDES = 2
STRAIGHT = ROWS - SIDEWAYS
STARTS = tuple(SIDEWAYS + sum(CHUNKS[:n]) for n in range(len(CHUNKS)))
NCHUNK = len(CHUNKS)
AHEAD = 2
FIRST_LAG = 1
SECOND_LAG = 2
SIDE_LAGS = (2, 4)
STACK_STEPS = tuple((dy, dc) for dy in (2, 1, 3, 0) for dc in (0, 1) if (dy, dc) != (0, 0))
ACROSS_STEPS = tuple((dx, dc) for dx in (2, 1, 3, 0) for dc in (0, 1) if (dx, dc) != (0, 0))
NT = (((1,), (1,)), ((), ()))


def body(
    angles, groups, class_row, group_row, chance_rows, particles, left_hbm, right_hbm, ctf_hbm,
    sums_out, weights_out, norms_out,
    left, right, ctf, images, weighted, power, outgoing, gathered,
    hot, hot_x, mixed, tile, posterior, tiles, tiles_x, norm_tile, norm_tiles,
    partial, first_in, second, second_in,
    small, small_first, small_mid, small_second, staged, side_second_in, side_third, side_third_in,
    load_sem, image_sem, own_sem,
    tile_send, tile_recv, norm_send, norm_recv,
    early_send, early_recv, y_send, y_recv,
    first_send, first_recv, second_send, second_recv,
    small_send, small_recv, result_sem,
    across_send, across_recv, tile_x_send, tile_x_recv, side_send, side_recv, side_own_sem,
):
    s = lax.axis_index("stack")
    k = lax.axis_index("cls")
    y, core = s // 2, s % 2
    z, x = k // 4, k % 4

    def along_stack(step):
        return (((y + step[0]) % 4) * 2 + (core + step[1]) % 2, k)

    def across(side, step):
        there = (z * 4 + (x + step[0]) % 4, ((z + step[0]) % 4) * 4 + x)[side]
        return (y * 2 + (core + step[1]) % 2, there)

    def along_x(d):
        return (s, z * 4 + (x + d) % 4)

    def along_z(d):
        return (s, ((z + d) % 4) * 4 + x)

    def along_y(d):
        return (((y + d) % 4) * 2 + core, k)

    wide, deep = (x, z), (z, x)
    along_wide, along_deep = (along_x, along_z), (along_z, along_x)

    def spread_at(side):
        return wide[side] * 2 + core


    loads = [
        pltpu.make_async_copy(left_hbm, left, load_sem.at[0]),
        pltpu.make_async_copy(right_hbm, right, load_sem.at[1]),
        pltpu.make_async_copy(ctf_hbm, ctf, load_sem.at[2]),
    ]

    def image_load(b):
        return pltpu.make_async_copy(
            particles.at[pl.ds(b * BATCH, BATCH)], images.at[b % 2], image_sem.at[b % 2]
        )

    loads[1].start()
    image_load(0).start()
    loads[0].start()
    loads[2].start()
    image_load(1).start()

    labels = jnp.concatenate(
        [class_row[...].astype(F32), group_row[...].astype(F32), chance_rows[...].astype(F32)], axis=0
    )
    tile[0:4, :] = jnp.concatenate([labels, labels], axis=1)
    tile[4:8, :] = jnp.zeros((4, LANES), F32)
    to_scalars = pltpu.make_async_copy(tile, posterior, load_sem.at[3])
    to_scalars.start()

    barrier = pltpu.get_barrier_semaphore()
    peers = [along_stack(step) for step in STACK_STEPS]
    for side in range(SIDES):
        peers += [across(side, step) for step in ACROSS_STEPS if step[0] != 0 and step[1] != 0]
    peers += [along_x(d) for d in (1, 2, 3)] + [along_z(d) for d in (1, 2, 3)]
    for peer in peers:
        pl.semaphore_signal(barrier, inc=1, device_id=peer, device_id_type=MESH)

    def remote(src, dst, send, recv, peer):
        return pltpu.make_async_remote_copy(
            src_ref=src, dst_ref=dst, send_sem=send, recv_sem=recv, device_id=peer, device_id_type=MESH
        )

    def tile_copies():
        return [
            remote(tile, tiles.at[s], tile_send.at[n], tile_recv.at[n], along_stack(step))
            for n, step in enumerate(STACK_STEPS)
        ]

    def tile_x_copies():
        return [
            remote(
                tile, tiles_x.at[side, spread_at(side)],
                tile_x_send.at[side, n], tile_x_recv.at[side, n], across(side, step),
            )
            for side in range(SIDES)
            for n, step in enumerate(ACROSS_STEPS)
        ]

    def sideways(side, spot):
        return side * STACK * 4 + spot * 4

    def across_copies(b):
        out = []
        for n, step in enumerate(ACROSS_STEPS):
            for side in range(SIDES):
                spot = ((wide[side] + step[0]) % 4) * 2 + (core + step[1]) % 2
                out.append(
                    remote(
                        outgoing.at[pl.ds(sideways(side, spot), 4), pl.ds(b * BATCH, BATCH)],
                        gathered.at[spread_at(side), pl.ds(side * 4, 4), pl.ds(b * BATCH, BATCH)],
                        across_send.at[b, side, n], across_recv.at[b, side, n], across(side, step),
                    )
                )
        return out

    def across_own(side):
        return pltpu.make_async_copy(
            outgoing.at[pl.ds(sideways(side, spread_at(side)), 4)],
            gathered.at[spread_at(side), pl.ds(side * 4, 4)],
            side_own_sem.at[side],
        )

    def side_first(side):
        rows = pl.ds(side * 4, 4)
        return [
            remote(
                partial.at[(deep[side] + d) % 4, rows], first_in.at[d - 1, rows],
                side_send.at[side, 0, d - 1], side_recv.at[side, 0, d - 1], along_deep[side](d),
            )
            for d in (1, 2, 3)
        ]

    def side_second(side):
        return [
            remote(
                second.at[:, pl.ds(side * 4 + (y + d) % 4, 1)], side_second_in.at[side, d - 1],
                side_send.at[side, 1, d - 1], side_recv.at[side, 1, d - 1], along_y(d),
            )
            for d in (1, 2, 3)
        ]

    def side_last(side):
        return [
            remote(
                side_third.at[side, (wide[side] + d) % 4], side_third_in.at[side, d - 1],
                side_send.at[side, 2, d - 1], side_recv.at[side, 2, d - 1], along_wide[side](d),
            )
            for d in (1, 2, 3)
        ]

    def norm_copies():
        return [
            remote(norm_tile, norm_tiles.at[s], norm_send.at[n], norm_recv.at[n], along_stack(step))
            for n, step in enumerate(STACK_STEPS)
        ]

    def straight(block, row):
        return STACK * SIDEWAYS + block * STRAIGHT + row - SIDEWAYS

    def early_copies(b):
        rows = CHUNKS[0]
        out = []
        for n, step in enumerate(STACK_STEPS):
            peer = along_stack(step)
            out.append(
                remote(
                    outgoing.at[pl.ds(straight(peer[0], STARTS[0]), rows), pl.ds(b * BATCH, BATCH)],
                    gathered.at[s, pl.ds(STARTS[0], rows), pl.ds(b * BATCH, BATCH)],
                    early_send.at[b, n], early_recv.at[b, n], peer,
                )
            )
        return out

    def y_copies(c):
        start, rows = STARTS[c], CHUNKS[c]
        out = []
        for n, step in enumerate(STACK_STEPS):
            peer = along_stack(step)
            out.append(
                remote(
                    outgoing.at[pl.ds(straight(peer[0], start), rows)],
                    gathered.at[s, pl.ds(start, rows)],
                    y_send.at[c, n], y_recv.at[c, n], peer,
                )
            )
        return out

    def own_copy(c):
        start, rows = STARTS[c], CHUNKS[c]
        return pltpu.make_async_copy(
            outgoing.at[pl.ds(straight(s, start), rows)],
            gathered.at[s, pl.ds(start, rows)],
            own_sem.at[c],
        )

    def first_copies(c):
        half = CHUNKS[c] // 2
        out = []
        for d in (1, 2, 3):
            for part, (hop, spot) in enumerate(((along_x, (x + d) % 4), (along_z, (z + d) % 4))):
                rows = pl.ds(STARTS[c] + part * half, half)
                out.append(
                    remote(
                        partial.at[spot, rows], first_in.at[d - 1, rows],
                        first_send.at[c, part, d - 1], first_recv.at[c, part, d - 1], hop(d),
                    )
                )
        return out

    def second_copies(c):
        half = CHUNKS[c] // 2
        out = []
        for d in (1, 2, 3):
            for part, (hop, spot) in enumerate(((along_z, (z + d) % 4), (along_x, (x + d) % 4))):
                rows = pl.ds(STARTS[c] + part * half, half)
                out.append(
                    remote(
                        second.at[spot, rows], second_in.at[d - 1, pl.ds(STARTS[c] - SIDEWAYS + part * half, half)],
                        second_send.at[c, part, d - 1], second_recv.at[c, part, d - 1], hop(d),
                    )
                )
        return out

    def small_first_copies():
        return [
            remote(
                small.at[pl.ds(((x + d) % 4) * 128, 128)], small_first.at[d - 1],
                small_send.at[0, d - 1], small_recv.at[0, d - 1], along_x(d),
            )
            for d in (1, 2, 3)
        ]

    def small_second_copies():
        return [
            remote(
                small_mid.at[pl.ds(((z + d) % 4) * CLS_LOC, CLS_LOC)], small_second.at[d - 1],
                small_send.at[1, d - 1], small_recv.at[1, d - 1], along_z(d),
            )
            for d in (1, 2, 3)
        ]

    def start(copies):
        for copy in copies:
            copy.start()

    def arrive(copies):
        for copy in copies:
            copy.wait_recv()

    def leave(copies):
        for copy in copies:
            copy.wait_send()

    for b in range(BATCHES):
        if b == 0:
            loads[1].wait()
        image_load(b).wait()
        if b == 0:
            loads[0].wait()
            loads[2].wait()
            to_scalars.wait()

        def several(n, carry, b=b):
            spots = [n * TOGETHER + m for m in range(TOGETHER)]
            turns, sheared = [], []
            for i in spots:
                turn = angles[b * BATCH + i]
                turns.append((turn, (turn + 1) & (ANGLES - 1)))
            for i, near in zip(spots, turns):
                image = images[b % 2, i]
                sheared.append([
                    lax.dot_general(image, right[turn], NT, preferred_element_type=F32).astype(BF16)
                    for turn in near
                ])
            for i, near, pair in zip(spots, turns, sheared):
                p = b * BATCH + i
                spun = posterior[2, p] * jnp.dot(left[near[0]], pair[0], preferred_element_type=F32)
                spun += posterior[3, p] * jnp.dot(left[near[1]], pair[1], preferred_element_type=F32)
                spun = ctf[groups[p]] * spun
                weighted[0, pl.ds(i * PITCH, SIDE), :] = spun[:, :LANES]
                weighted[1, pl.ds(i * PITCH, SIDE), :] = spun[:, LANES:]
                squares = jnp.sum(spun * spun, axis=0, keepdims=True)
                power[pl.ds(p, 1), :] = squares[:, :LANES] + squares[:, LANES:]
            return carry

        lax.fori_loop(0, BATCH // TOGETHER, several, 0)
        if b + 2 < BATCHES:
            image_load(b + 2).start()

        def turn_over(block, carry, b=b):
            for r in range(ROWS):
                if r < SIDEWAYS:
                    place = sideways(r // 4, (r % 4) * 2 + (block & 1)) + (block >> 1)
                else:
                    place = straight(block, r)
                for h in range(2):
                    lines = weighted[h, pl.ds(block * ROWS + r, BATCH, stride=PITCH), :]
                    outgoing[place, b * BATCH:(b + 1) * BATCH, h * LANES:(h + 1) * LANES] = lines.astype(BF16)
            return carry

        lax.fori_loop(0, STACK, turn_over, 0)
        if b == 0:
            pl.semaphore_wait(barrier, len(peers))
            start(tile_copies())
            start(tile_x_copies())
        start(across_copies(b))
        start(early_copies(b))

    for c in range(1, AHEAD):
        start(y_copies(c))
    for c in range(NCHUNK):
        own_copy(c).start()

    for side in range(SIDES):
        across_own(side).start()

    tiles[s] = tile[...]
    for side in range(SIDES):
        tiles_x[side, spread_at(side)] = tile[...]
    lane = lax.broadcasted_iota(jnp.int32, (8, LANES), 1)
    own_power = jnp.sum(power[...], axis=1, keepdims=True) * (1.0 / (SIDE * SIDE))
    spot = lax.broadcasted_iota(jnp.int32, (LOCAL, LANES), 1) & (LOCAL - 1)
    line = lax.broadcasted_iota(jnp.int32, (LOCAL, LANES), 0)
    own_power = jnp.sum(jnp.where(spot == line, own_power, 0.0), axis=0, keepdims=True)
    norm_tile[...] = jnp.broadcast_to(own_power, (8, LANES))
    norm_tiles[s] = jnp.broadcast_to(own_power, (8, LANES))
    start(norm_copies())

    arrive(tile_copies())
    arrive(tile_x_copies())
    natural = lax.broadcasted_iota(jnp.int32, (CLASSES, LANES), 0).astype(F32)
    which = lax.broadcasted_iota(jnp.int32, (LANES, LANES), 0)
    which_group = (which & (GROUPS - 1)).astype(F32)
    for j in range(STACK // 2):
        cols = slice(j * LANES, (j + 1) * LANES)
        both = jnp.where(lane < LOCAL, tiles[2 * j], tiles[2 * j + 1])
        hot[:, cols] = jnp.where(natural == both[0:1], 1.0, 0.0).astype(BF16)
        for side in range(SIDES):
            beside = jnp.where(lane < LOCAL, tiles_x[side, 2 * j], tiles_x[side, 2 * j + 1])
            hot_x[side, :, cols] = jnp.where(natural == beside[0:1], 1.0, 0.0).astype(BF16)
        chance = jnp.where(which < GROUPS, both[2:3], both[3:4])
        keep = (which_group == both[1:2]) & (which < 2 * GROUPS)
        mixed[:, cols] = jnp.where(keep, chance, 0.0).astype(BF16)

    def keep_lines(which, r, lines):
        at = pl.ds(pl.multiple_of((which * ROWS + r) * CLS_LOC, CLS_LOC), CLS_LOC)
        weighted[0, at, :] = lines[:, :LANES]
        weighted[1, at, :] = lines[:, LANES:]

    def result_copy(which, block):
        rows = pl.ds(block * 8, 8)
        target = (sums_out, weights_out)[which]
        return pltpu.make_async_copy(
            staged.at[which, :, rows], target.at[:, rows], result_sem.at[which, block]
        )

    def settle(which, block):
        def one_class(i, carry):
            for h in range(2):
                at = pl.ds((which * ROWS + block * 8) * CLS_LOC + i, 8, stride=CLS_LOC)
                staged[which, i, block * 8:block * 8 + 8, h * LANES:(h + 1) * LANES] = weighted[h, at, :]
            return carry

        lax.fori_loop(0, CLS_LOC, one_class, 0, unroll=8)
        result_copy(which, block).start()

    def small_start():
        arrive(norm_copies())
        total = jnp.zeros((CLASSES, LANES), F32)
        for j in range(STACK // 2):
            both = jnp.where(lane < LOCAL, tiles[2 * j], tiles[2 * j + 1])
            norm = jnp.where(lane < LOCAL, norm_tiles[2 * j], norm_tiles[2 * j + 1])
            total += jnp.where(natural == both[0:1], norm[0:1], 0.0)
        blend = lax.dot_general(hot[...], mixed[...], NT, preferred_element_type=F32)
        for owner in range(OWNERS):
            line = ((owner % 4) * 4 + owner // 4) * CLS_LOC
            small[line:line + CLS_LOC, 0:LANES] = total[owner * CLS_LOC:(owner + 1) * CLS_LOC]
            small[line:line + CLS_LOC, LANES:2 * LANES] = blend[owner * CLS_LOC:(owner + 1) * CLS_LOC]
        start(small_first_copies())

    def small_middle():
        arrive(small_first_copies())
        small_mid[...] = (
            small[pl.ds(x * 128, 128), :] + small_first[0] + small_first[1] + small_first[2]
        )
        start(small_second_copies())

    def small_end():
        arrive(small_second_copies())
        total = small_mid[pl.ds(z * CLS_LOC, CLS_LOC), :] + small_second[0] + small_second[1] + small_second[2]
        norms = jnp.sum(total[:, :LANES], axis=1, keepdims=True)
        lined = lax.broadcasted_iota(jnp.int32, (CLS_LOC, LANES), 0)
        lined = lined == lax.broadcasted_iota(jnp.int32, (CLS_LOC, LANES), 1)
        norms_out[...] = jnp.sum(jnp.where(lined, norms, 0.0), axis=0, keepdims=True)
        coef = total[:, LANES:LANES + GROUPS] + total[:, LANES + GROUPS:LANES + 2 * GROUPS]

        def weigh(r, carry):
            lines = jnp.concatenate([ctf[g, pl.ds(s * ROWS + r, 1), :] for g in range(GROUPS)], axis=0)
            spread = jnp.dot(
                coef, lines * lines, precision=lax.Precision.HIGHEST, preferred_element_type=F32
            )
            keep_lines(1, r, spread)
            return carry

        lax.fori_loop(0, ROWS, weigh, 0)
        for block in range(ROWS // 8):
            settle(1, block)

    def keep_partial(part, r, sums):
        if part == 0:
            for owner in range(OWNERS):
                line = (owner // 4) * CLS_LOC
                block = sums[owner * CLS_LOC:(owner + 1) * CLS_LOC]
                partial[owner % 4, r, line:line + CLS_LOC, :] = block
        else:
            partial[:, r] = sums.reshape(4, 128, SIDE)

    def by_class(c):
        half = CHUNKS[c] // 2
        for part in range(2):

            def add(i, carry, part=part):
                r = STARTS[c] + part * half + i
                lines = gathered[:, r].reshape(PEOPLE, SIDE)
                sums = jnp.dot(hot[...], lines, preferred_element_type=F32).astype(BF16)
                keep_partial(part, r, sums)
                return carry

            lax.fori_loop(0, half, add, 0)

    def add_first(c):
        half = CHUNKS[c] // 2
        for part, mine in enumerate((x, z)):

            def add(i, carry, part=part, mine=mine):
                r = STARTS[c] + part * half + i
                total = partial[mine, r].astype(F32)
                for d in range(3):
                    total += first_in[d, r].astype(F32)
                second[:, r] = total.reshape(4, CLS_LOC, SIDE)
                return carry

            lax.fori_loop(0, half, add, 0)

    def add_second(c):
        half = CHUNKS[c] // 2
        for part, mine in enumerate((z, x)):

            def add(i, carry, part=part, mine=mine):
                r = STARTS[c] + part * half + i
                total = second[mine, r]
                for d in range(3):
                    total += second_in[d, r - SIDEWAYS]
                keep_lines(0, r, total)
                return carry

            lax.fori_loop(0, half, add, 0)

    def side_by_class(side):
        def add(i, carry):
            r = side * 4 + i
            lines = gathered[:, r].reshape(PEOPLE, SIDE)
            sums = jnp.dot(hot_x[side], lines, preferred_element_type=F32).astype(BF16)
            keep_partial(1 - side, r, sums)
            return carry

        lax.fori_loop(0, 4, add, 0)

    def side_add_first(side):
        def add(i, carry):
            r = side * 4 + i
            total = partial[deep[side], r].astype(F32)
            for d in range(3):
                total += first_in[d, r].astype(F32)
            second[:, r] = total.reshape(4, CLS_LOC, SIDE)
            return carry

        lax.fori_loop(0, 4, add, 0)

    def side_add_second(side):
        for block in range(4):
            total = second[block, side * 4 + y]
            for d in range(3):
                total += side_second_in[side, d, block, 0]
            side_third[side, block] = total

    def side_keep(side):
        keep_lines(0, side * 4 + wide[side], side_third[side, wide[side]])
        for d in (1, 2, 3):
            keep_lines(0, side * 4 + (wide[side] + 4 - d) % 4, side_third_in[side, d - 1])

    for c in range(NCHUNK + SECOND_LAG):
        if c < NCHUNK:
            if c == 0:
                for b in range(BATCHES):
                    arrive(early_copies(b))
            else:
                arrive(y_copies(c))
            if c + AHEAD < NCHUNK:
                start(y_copies(c + AHEAD))
            own_copy(c).wait()
            by_class(c)
            start(first_copies(c))
        if c == 0:
            for b in range(BATCHES):
                arrive(across_copies(b))
            for side in range(SIDES):
                across_own(side).wait()
                side_by_class(side)
                start(side_first(side))
        if c == SIDE_LAGS[0]:
            for side in range(SIDES):
                arrive(side_first(side))
                side_add_first(side)
                start(side_second(side))
        if c == SIDE_LAGS[1]:
            for side in range(SIDES):
                arrive(side_second(side))
                side_add_second(side)
                start(side_last(side))
        if c == NCHUNK:
            for side in range(SIDES):
                arrive(side_last(side))
                side_keep(side)
            settle(0, 0)
        if c == 0:
            small_start()
        if c == 1:
            small_middle()
        if 0 <= c - FIRST_LAG < NCHUNK:
            arrive(first_copies(c - FIRST_LAG))
            add_first(c - FIRST_LAG)
            start(second_copies(c - FIRST_LAG))
        if c == 2:
            small_end()
        if 0 <= c - SECOND_LAG < NCHUNK:
            arrive(second_copies(c - SECOND_LAG))
            add_second(c - SECOND_LAG)
            begun = STARTS[c - SECOND_LAG]
            for block in range(begun // 8, (begun + CHUNKS[c - SECOND_LAG]) // 8):
                settle(0, block)

    leave(tile_copies())
    leave(norm_copies())
    for b in range(BATCHES):
        leave(early_copies(b))
    for c in range(NCHUNK):
        if c > 0:
            leave(y_copies(c))
        leave(first_copies(c))
        leave(second_copies(c))
    leave(small_first_copies())
    leave(small_second_copies())
    leave(tile_x_copies())
    for b in range(BATCHES):
        leave(across_copies(b))
    for side in range(SIDES):
        leave(side_first(side))
        leave(side_second(side))
        leave(side_last(side))
    for which in range(2):
        for block in range(ROWS // 8):
            result_copy(which, block).wait()


def hand_over(sums, weights, norms, sums_out, weights_out, norms_out, held, in_sem, out_sem):
    size = CLS_LOC // PIECES
    arriving, leaving = [], []
    for n in range(PIECES):
        part = pl.ds(n * size, size)
        for which, (src, dst) in enumerate(((sums, sums_out), (weights, weights_out))):
            arriving.append(pltpu.make_async_copy(src.at[part], held.at[which, part], in_sem.at[which, n]))
            leaving.append(pltpu.make_async_copy(held.at[which, part], dst.at[part], out_sem.at[which, n]))
    for copy in arriving:
        copy.start()
    norms_out[...] = norms[0, :CLS_LOC]
    for here, there in zip(arriving, leaving):
        here.wait()
        there.start()
    for copy in leaving:
        copy.wait()


def per_device(particles, classes, angles, groups, posterior, left_maps, right_maps, ctf_table):
    smem = pl.BlockSpec(memory_space=pltpu.SMEM)
    vmem = pl.BlockSpec(memory_space=pltpu.VMEM)
    hbm = pl.BlockSpec(memory_space=pl.ANY)
    n = len(STACK_STEPS)
    dma = pltpu.SemaphoreType.DMA
    sums, weights, norms = pl.pallas_call(
        body,
        out_shape=(
            jax.ShapeDtypeStruct((CLS_LOC, ROWS, SIDE), F32),
            jax.ShapeDtypeStruct((CLS_LOC, ROWS, SIDE), F32),
            jax.ShapeDtypeStruct((1, LANES), F32),
        ),
        in_specs=[smem, smem, vmem, vmem, vmem, hbm, hbm, hbm, hbm],
        out_specs=(hbm, hbm, vmem),
        scratch_shapes=[
            pltpu.VMEM((ANGLES, SIDE, SIDE), BF16),
            pltpu.VMEM((ANGLES, SIDE, SIDE), BF16),
            pltpu.VMEM((GROUPS, SIDE, SIDE), F32),
            pltpu.VMEM((2, BATCH, SIDE, SIDE), BF16),
            pltpu.VMEM((2, BATCH * PITCH, LANES), F32),
            pltpu.VMEM((LOCAL, LANES), F32),
            pltpu.VMEM((SIDE, LOCAL, SIDE), BF16),
            pltpu.VMEM((STACK, ROWS, LOCAL, SIDE), BF16),
            pltpu.VMEM((CLASSES, PEOPLE), BF16),
            pltpu.VMEM((SIDES, CLASSES, PEOPLE), BF16),
            pltpu.VMEM((LANES, PEOPLE), BF16),
            pltpu.VMEM((8, LANES), F32),
            pltpu.SMEM((8, LANES), F32),
            pltpu.VMEM((STACK, 8, LANES), F32),
            pltpu.VMEM((SIDES, STACK, 8, LANES), F32),
            pltpu.VMEM((8, LANES), F32),
            pltpu.VMEM((STACK, 8, LANES), F32),
            pltpu.VMEM((4, ROWS, 128, SIDE), BF16),
            pltpu.VMEM((3, ROWS, 128, SIDE), BF16),
            pltpu.VMEM((4, ROWS, CLS_LOC, SIDE), F32),
            pltpu.VMEM((3, STRAIGHT, CLS_LOC, SIDE), F32),
            pltpu.VMEM((CLASSES, 2 * LANES), F32),
            pltpu.VMEM((3, 128, 2 * LANES), F32),
            pltpu.VMEM((128, 2 * LANES), F32),
            pltpu.VMEM((3, CLS_LOC, 2 * LANES), F32),
            pltpu.VMEM((2, CLS_LOC, ROWS, SIDE), F32),
            pltpu.VMEM((SIDES, 3, 4, 1, CLS_LOC, SIDE), F32),
            pltpu.VMEM((SIDES, 4, CLS_LOC, SIDE), F32),
            pltpu.VMEM((SIDES, 3, CLS_LOC, SIDE), F32),
            dma((4,)), dma((2,)), dma((NCHUNK,)),
            dma((n,)), dma((n,)), dma((n,)), dma((n,)),
            dma((BATCHES, n)), dma((BATCHES, n)), dma((NCHUNK, n)), dma((NCHUNK, n)),
            dma((NCHUNK, 2, 3)), dma((NCHUNK, 2, 3)), dma((NCHUNK, 2, 3)), dma((NCHUNK, 2, 3)),
            dma((2, 3)), dma((2, 3)), dma((2, ROWS // 8)),
            dma((BATCHES, SIDES, n)), dma((BATCHES, SIDES, n)), dma((SIDES, n)), dma((SIDES, n)),
            dma((SIDES, 3, 3)), dma((SIDES, 3, 3)), dma((SIDES,)),
        ],
        compiler_params=pltpu.CompilerParams(
            collective_id=0, has_side_effects=True, vmem_limit_bytes=63 * 1024 * 1024
        ),
        name="class_sums",
    )(angles, groups, classes.reshape(1, LOCAL), groups.reshape(1, LOCAL), posterior.T, particles, left_maps, right_maps, ctf_table)
    shape = jax.ShapeDtypeStruct((CLS_LOC, ROWS, SIDE), F32)
    return pl.pallas_call(
        hand_over,
        out_shape=(shape, shape, jax.ShapeDtypeStruct((CLS_LOC,), F32)),
        in_specs=[hbm, hbm, vmem],
        out_specs=(hbm, hbm, vmem),
        scratch_shapes=[pltpu.VMEM((2, CLS_LOC, ROWS, SIDE), F32), dma((2, PIECES)), dma((2, PIECES))],
        compiler_params=pltpu.CompilerParams(vmem_limit_bytes=63 * 1024 * 1024),
        name="hand_over",
    )(sums, weights, norms)


def solution(mesh):
    return jax.shard_map(
        per_device,
        mesh=mesh,
        in_specs=(
            P(("stack", "cls"), None, None),
            P(("stack", "cls")),
            P(("stack", "cls")),
            P(("stack", "cls")),
            P(("stack", "cls"), None),
            P(),
            P(),
            P(),
        ),
        out_specs=(P("cls", "stack", None), P("cls", "stack", None), P("cls")),
        check_vma=False,
    )
```
